32 devices in a mesh: nodes: 8 (over z, y), feat: 4 (over x, core).
Axes of the slice: x: 2, y: 2, z: 4, core: 2. Of those that a mesh axis runs over, the one named last changes fastest.
Arguments:
- features: bfloat16 [8192, 1024], P('nodes', 'feat'), may hold values from -6 to 6
- ghosts: int32 [64, 2], P('nodes'), may hold values from 0 to 7, as said below
- slots: int32 [64, 24], P('nodes'), may hold values from 0 to 15
- tile_ids: int32 [64, 24], P('nodes'), may hold values from 0 to 15
- degrees: int32 [64], P('nodes'), may hold values from 1 to 24, 512 in all
- tile_table: bfloat16 [16, 128, 128], replicated, may hold values from -0.5 to 0.5
- weight_one: bfloat16 [1024, 1024], P(None, 'feat'), may hold values from -0.1875 to 0.1875
- weight_two: bfloat16 [1024, 1024], P(None, 'feat'), may hold values from -0.1875 to 0.1875
- cotangent: bfloat16 [8192, 1024], P('nodes', 'feat'), may hold values from -0.15625 to 0.15625
Outputs:
- output: bfloat16 [8192, 1024], P('nodes', 'feat')
- grad_one: float32 [1024, 1024], P('nodes', 'feat')
- grad_two: float32 [1024, 1024], P('nodes', 'feat')
The draws below stay inside these ranges and needn't reach their ends.
Inputs may be any that keep to these rules, and one draw needn't show every extreme that they name: `ghosts`: row d * 8 + p holds 2 distinct block indices of device p. The degrees sum to 512; the largest is 24.
All inputs are finite; a program needn't handle non-finite values. No bound on the sum of `degrees` on one device may be relied on, other than what follows from the above.
Results may differ from the reference program's by a relative error of at most 0.0061.
Values may be sent and summed in bfloat16 or wider, within the bound.
No kernel may reach another device: no remote copies, remote signals or barrier semaphores. Data moves between devices by JAX's collectives and lax.ppermute only.
A program may use at most 64 MiB of HBM per device.

```python
import math
import jax
import jax.numpy as jnp
import numpy as np
from jax import lax

H = 1024
BS = 128
BLK_DEV = 8
GHOST = 2
KMAX = 24
DEG = 8
NTAB = 16
NB = 64
NODES = 8192
SLOTS = 16
N_NODES = 8


def draw_ghosts(key, part):
    pair_rows = N_NODES * N_NODES
    scores = jax.random.randint(key, (pair_rows, BLK_DEV), 0, 1 << 20) * BLK_DEV
    scores = scores + jnp.arange(BLK_DEV, dtype=jnp.int32)[None, :]
    ranking = jnp.argsort(scores, axis=1, stable=True)
    return ranking[:, :GHOST].astype(jnp.int32)


def place_ends(values, rng, low, largest):
    index_at = [jax.random.randint(jax.random.fold_in(rng, axis), (), 0, length) for axis, length in enumerate(values.shape)]
    widest = values.shape.index(max(values.shape))
    next_to = index_at[:widest] + [(index_at[widest] + 1) % values.shape[widest]] + index_at[widest + 1:]
    return values.at[tuple(index_at)].set(low).at[tuple(next_to)].set(largest)


def level_of(rng, shape, pieces, low, high):
    gain = 1.0
    for dim, shards_of in pieces:
        heights = jax.random.uniform(jax.random.fold_in(jax.random.fold_in(rng, 6), dim), (shards_of,), jnp.float32, low / len(pieces), high / len(pieces))
        gain = gain * jnp.repeat(jnp.exp(heights), shape[dim] // shards_of).reshape((-1,) + (1,) * (len(shape) - 1 - dim))
    return gain


def length_profile(count, total, limit, slope):
    loads = [(1 << 20) // math.isqrt(rank ** slope) + 1 for rank in range(2, count + 1)]
    rest, holding = total - limit - (count - 1), [1] * (count - 1)
    while rest > 0:
        free = [i for i in range(count - 1) if holding[i] < limit]
        mass, remaining = sum([loads[i] for i in free]), rest
        for i in free:
            more = min(limit - holding[i], max(1, remaining * loads[i] // mass), rest)
            holding[i] = holding[i] + more
            rest = rest - more
    return np.array([limit] + holding)


def ragged_sizes(key, amount, total, reach, slope):
    if amount == 2:
        one = jax.random.randint(key, (), max(1, total - reach), min(reach, total - 1) + 1)
        return jnp.stack([one, total - one])
    lengths = jnp.asarray(length_profile(amount, total, reach, slope), jnp.int32)
    twos = (amount - 1) // 2
    giver, sink = lengths[1:1 + 2 * twos:2], lengths[2:2 + 2 * twos:2]
    room = jnp.minimum(giver - 1, reach - sink)
    moved = jax.random.randint(jax.random.fold_in(key, 1), (twos,), 0, 1 << 20) % (room + 1)
    lengths = lengths.at[1:1 + 2 * twos:2].set(giver - moved).at[2:2 + 2 * twos:2].set(sink + moved)
    return lengths[jax.random.permutation(jax.random.fold_in(key, 2), amount)]


def normal_values(key, shape, scale, bound, shards=(), held_as=jnp.bfloat16):
    loudness = level_of(key, shape, shards, -0.22, 0.18) if shards else 1.0
    array = jax.random.normal(key, shape, jnp.float32) * scale * loudness
    return jnp.minimum(jnp.maximum(array, -bound), bound).astype(held_as)


def setup_inputs(seed: int = 0) -> dict:
    keys = jax.random.split(jax.random.key(seed), 10)
    features = normal_values(keys[0], (NODES, H), 1.0, 6.0, ((0, 8), (1, 4)))
    ghosts = draw_ghosts(jax.random.fold_in(keys[9], 71), 0)
    slots = place_ends(jax.random.randint(keys[2], (NB, KMAX), 0, SLOTS), jax.random.fold_in(keys[2], 1), 0, SLOTS - 1).astype(jnp.int32)
    tile_ids = place_ends(jax.random.randint(keys[3], (NB, KMAX), 0, NTAB), jax.random.fold_in(keys[3], 1), 0, NTAB - 1).astype(jnp.int32)
    degrees = ragged_sizes(keys[4], NB, NB * DEG, KMAX, 2).astype(jnp.int32)
    tile_table = normal_values(keys[5], (NTAB, BS, BS), BS ** -0.5, 0.5)
    weight_one = normal_values(keys[6], (H, H), H ** -0.5, 0.1875, ((1, 4),))
    weight_two = normal_values(keys[7], (H, H), H ** -0.5, 0.1875, ((1, 4),))
    cotangent = normal_values(keys[8], (NODES, H), 0.01, 0.15625, ((0, 8), (1, 4)))
    return {"features": features, "ghosts": ghosts, "slots": slots, "tile_ids": tile_ids, "degrees": degrees, "tile_table": tile_table, "weight_one": weight_one, "weight_two": weight_two, "cotangent": cotangent}


def ghost_index(ghosts, slots):
    owner_dev = jnp.arange(NB, dtype=jnp.int32) // BLK_DEV
    peer_dev = slots // GHOST
    column = slots % GHOST
    local_block = ghosts[owner_dev[:, None] * N_NODES + peer_dev, column]
    return (peer_dev * BLK_DEV + local_block).astype(jnp.int32)

def entry_weights(degrees):
    position = jnp.arange(KMAX, dtype=jnp.int32)[None, :]
    inverse_root = lax.rsqrt(degrees.astype(jnp.float32))[:, None]
    return jnp.where(position < degrees[:, None], inverse_root, jnp.zeros_like(inverse_root))

def propagate(values, neighbour, tile_ids, weights, tile_table):
    grouped = values.reshape(NB, BS, values.shape[1])
    tile_rows = tile_table.astype(jnp.float32)

    def one_block(block_args):
        row_nb, row_tiles, row_weights, own_block = block_args
        near_rows = grouped[row_nb]
        picked = tile_rows[row_tiles]
        products = jnp.einsum('kij,kjf->kif', picked, near_rows, precision=lax.Precision.HIGHEST)
        return own_block + jnp.einsum('k,kif->if', row_weights, products, precision=lax.Precision.HIGHEST)
    result = lax.map(one_block, (neighbour, tile_ids, weights, grouped))
    return result.reshape(values.shape)

def back_spread(grad_agg, ghosts, slots, tile_ids, weights, tile_table):
    width = grad_agg.shape[1]
    grouped = grad_agg.astype(jnp.float32).reshape(NB, BS, width)
    tile_rows = tile_table.astype(jnp.float32)
    slot_ids = jnp.arange(SLOTS, dtype=jnp.int32)
    peer_dev = slot_ids // GHOST
    column = slot_ids % GHOST

    def one_device(carry, device):
        first = (device * BLK_DEV).astype(jnp.int32)
        dev_blocks = lax.dynamic_slice_in_dim(grouped, first, BLK_DEV, 0)
        dev_slots = lax.dynamic_slice_in_dim(slots, first, BLK_DEV, 0)
        dev_tiles = lax.dynamic_slice_in_dim(tile_ids, first, BLK_DEV, 0)
        dev_weights = lax.dynamic_slice_in_dim(weights, first, BLK_DEV, 0)

        def one_block(partial_value, block_args):
            row_slots, row_tiles, row_weights, block = block_args
            products = jnp.einsum('kji,jf->kif', tile_rows[row_tiles], block, precision=lax.Precision.HIGHEST)
            scaled = row_weights[:, None, None] * products
            return (partial_value + jax.ops.segment_sum(scaled, row_slots, num_segments=SLOTS), None)
        start_value = jnp.zeros((SLOTS, BS, width), jnp.float32)
        partial_value, unused = lax.scan(one_block, start_value, (dev_slots, dev_tiles, dev_weights, dev_blocks))
        rounded = lax.optimization_barrier(partial_value.astype(jnp.bfloat16)).astype(jnp.float32)
        local_block = ghosts[device * N_NODES + peer_dev, column]
        target = (peer_dev * BLK_DEV + local_block).astype(jnp.int32)
        return (carry.at[target].add(rounded), None)
    total = jnp.zeros((NB, BS, width), jnp.float32)
    total, unused = lax.scan(one_device, total, jnp.arange(N_NODES, dtype=jnp.int32))
    return (grouped + total).reshape(grad_agg.shape)

def reference(features, ghosts, slots, tile_ids, degrees, tile_table, weight_one, weight_two, cotangent):
    neighbour = ghost_index(ghosts, slots)
    weights = entry_weights(degrees)

    def spread(field):
        return propagate(field, neighbour, tile_ids, weights, tile_table)
    agg_one = spread(features.astype(jnp.float32)).astype(jnp.bfloat16)
    pre_one = jnp.dot(agg_one, weight_one, preferred_element_type=jnp.float32)
    hidden = jax.nn.silu(pre_one).astype(jnp.bfloat16)
    agg_two = spread(hidden.astype(jnp.float32)).astype(jnp.bfloat16)
    output = jnp.dot(agg_two, weight_two, preferred_element_type=jnp.float32).astype(jnp.bfloat16)
    grad_two = jnp.dot(agg_two.T, cotangent, preferred_element_type=jnp.float32)
    grad_agg = jnp.dot(cotangent, weight_two.T, preferred_element_type=jnp.float32).astype(jnp.bfloat16)
    back_hidden = back_spread(grad_agg, ghosts, slots, tile_ids, weights, tile_table)
    sigmoid_pre = jax.nn.sigmoid(pre_one)
    back_pre = (back_hidden * sigmoid_pre * (1.0 + pre_one * (1.0 - sigmoid_pre))).astype(jnp.bfloat16)
    grad_one = jnp.dot(agg_one.T, back_pre, preferred_element_type=jnp.float32)
    return (output, grad_one, grad_two)
```

```python
import functools

import jax
import jax.numpy as jnp
from jax import lax
from jax.experimental import pallas as pl
from jax.experimental.pallas import tpu as pltpu
from jax.sharding import PartitionSpec as P

unroll = 4
bf16, f32 = jnp.bfloat16, jnp.float32


def nt_dot(a, b):
    return lax.dot_general(a, b, (((1,), (1,)), ((), ())), preferred_element_type=f32)


def form_products(x_ref, tiles_ref, p_ref, transposed):
    count, width, size = x_ref.shape
    tile_count = tiles_ref.shape[0]
    group = min(count, max(1, 512 // width))

    def pair(turn, carry):
        two = tiles_ref[pl.ds(2 * turn, 2)]
        if transposed:
            right = jnp.concatenate([two[0], two[1]], axis=1)
        else:
            right = two.reshape(2 * size, size)
        for first in range(0, count, group):
            left = x_ref[first : first + group].reshape(group * width, size)
            if transposed:
                res = jnp.dot(left, right, preferred_element_type=f32)
            else:
                res = nt_dot(left, right)
            for half in range(2):
                part = res[:, half * size : (half + 1) * size].reshape(group, width, size)
                p_ref[pl.ds((2 * turn + half) * count + first, group)] = part
        return carry

    lax.fori_loop(0, tile_count // 2, pair, 0)
    p_ref[tile_count * count] = jnp.zeros((width, size), f32)


def load_blocks(v_ref, x_ref, form, per):
    size = x_ref.shape[2]
    if form == "N":
        for n in range(v_ref.shape[0]):
            for b in range(per):
                x_ref[n * per + b] = v_ref[n, :, b * size : (b + 1) * size]
    else:
        share = v_ref.shape[3] // size
        for f in range(v_ref.shape[0]):
            for n in range(v_ref.shape[1]):
                for j in range(share):
                    x_ref[n * per + f * share + j] = v_ref[f, n, :, j * size : (j + 1) * size]


def put_block(o_ref, form, n, b, value):
    size = value.shape[1]
    if form == "N":
        o_ref[n, :, b * size : (b + 1) * size] = value
    else:
        share = o_ref.shape[3] // size
        j = b % share
        o_ref[b // share, n, :, j * size : (j + 1) * size] = value


def spread_kernel(form_in, form_out, per, width_k, pick, trips, weight, v_ref, tiles_ref, o_ref, x_ref, p_ref):
    load_blocks(v_ref, x_ref, form_in, per)
    form_products(x_ref, tiles_ref, p_ref, False)
    count, width, size = x_ref.shape

    def device_rows(n, carry):
        for b in range(per):
            r = n * per + b

            def chunk(c, acc):
                base = r * width_k + c * unroll
                terms = [p_ref[pick[base + u]] for u in range(unroll)]
                return acc + ((terms[0] + terms[1]) + (terms[2] + terms[3]))

            acc = lax.fori_loop(0, trips[r], chunk, jnp.zeros((width, size), f32))
            put_block(o_ref, form_out, n, b, (x_ref[r].astype(f32) + weight[r] * acc).astype(bf16))
        return carry

    lax.fori_loop(0, count // per, device_rows, 0)


def back_kernel(
    form_in, form_out, per, width_k, pick, near, trips, weight, v_ref, tiles_ref, o_ref, x_ref, p_ref, *sums
):
    load_blocks(v_ref, x_ref, form_in, per)
    form_products(x_ref, tiles_ref, p_ref, True)
    count, width, size = x_ref.shape
    for u, total in enumerate(sums):
        total[...] = x_ref[...].astype(f32) if u == 0 else jnp.zeros(total.shape, f32)

    def row(r, carry):
        share = weight[r]

        def chunk(c, inner):
            base = r * width_k + c * unroll
            for u in range(unroll):
                g = near[base + u]
                sums[u][g] = sums[u][g] + share * p_ref[pick[base + u]]
            return inner

        return lax.fori_loop(0, trips[r], chunk, carry)

    lax.fori_loop(0, count, row, 0)

    def device_rows(n, carry):
        for b in range(per):
            r = n * per + b
            value = (sums[0][r] + sums[1][r]) + (sums[2][r] + sums[3][r])
            put_block(o_ref, form_out, n, b, value.astype(bf16))
        return carry

    lax.fori_loop(0, count // per, device_rows, 0)


def to_blocks(v, form, per, size):
    if form == "N":
        n, width = v.shape[0], v.shape[1]
        return v[:, :, : per * size].reshape(n, width, per, size).transpose(0, 2, 1, 3).reshape(n * per, width, size)
    f, n, width, _ = v.shape
    return v.reshape(f, n, width, per // f, size).transpose(1, 0, 3, 2, 4).reshape(n * per, width, size)


def from_blocks(x, form, per, feat_count):
    count, width, size = x.shape
    n = count // per
    if form == "N":
        return x.reshape(n, per, width, size).transpose(0, 2, 1, 3).reshape(n, width, per * size)
    share = per // feat_count
    return (
        x.reshape(n, feat_count, share, width, size)
        .transpose(1, 0, 3, 2, 4)
        .reshape(feat_count, n, width, share * size)
    )


def plain_spread(v, form_in, form_out, meta, tiles, feat_count, transposed):
    near, tile_ids, live, weight, per = meta["near"], meta["tile"], meta["live"], meta["weight"], meta["per"]
    x = to_blocks(v, form_in, per, tiles.shape[1])
    rows = jnp.arange(x.shape[0])
    kind = "gfi,tij->tgfj" if transposed else "gfj,tij->tgfi"
    products = jnp.einsum(kind, x, tiles, preferred_element_type=f32)

    def step(k, acc):
        g, t = near[:, k], tile_ids[:, k]
        share = jnp.where(live[:, k], weight, 0.0)[:, None, None]
        if transposed:
            return acc.at[g].add(share * products[t, rows])
        return acc + share * products[t, g]

    out = lax.fori_loop(0, near.shape[1], step, x.astype(f32)).astype(bf16)
    return from_blocks(out, form_out, per, feat_count)


def local_spread(v, form_in, form_out, meta, tiles, feat_count, transposed=False):
    width = v.shape[-2]
    if width % 16:
        return plain_spread(v, form_in, form_out, meta, tiles, feat_count, transposed)
    per, size = meta["per"], tiles.shape[1]
    count, width_k = meta["near"].shape
    if form_out == "N":
        shape = (count // per, width, per * size)
    else:
        shape = (feat_count, count // per, width, (per // feat_count) * size)
    smem = pl.BlockSpec(memory_space=pltpu.SMEM)
    vmem = pl.BlockSpec(memory_space=pltpu.VMEM)
    scratch = [
        pltpu.VMEM((count, width, size), bf16),
        pltpu.VMEM((tiles.shape[0] * count + 1, width, size), f32),
    ]
    if transposed:
        body = functools.partial(back_kernel, form_in, form_out, per, width_k)
        scalars = (meta["pick_back"], meta["near_flat"], meta["trips"], meta["weight"])
        scratch += [pltpu.VMEM((count, width, size), f32)] * unroll
    else:
        body = functools.partial(spread_kernel, form_in, form_out, per, width_k)
        scalars = (meta["pick"], meta["trips"], meta["weight"])
    return pl.pallas_call(
        body,
        out_shape=jax.ShapeDtypeStruct(shape, bf16),
        in_specs=[smem] * len(scalars) + [vmem, vmem],
        out_specs=vmem,
        scratch_shapes=scratch,
        compiler_params=pltpu.CompilerParams(vmem_limit_bytes=48 * 1024 * 1024),
        cost_estimate=pl.CostEstimate(
            flops=2 * tiles.shape[0] * count * width * size * size, bytes_accessed=16 << 20, transcendentals=0
        ),
    )(*scalars, v, tiles)


def pack_meta(ghosts, slots, tile_ids, degrees, width, size):
    per = slots.shape[0]
    held = ghosts.shape[1]
    peer = slots // held
    choice = jnp.arange(ghosts.size, dtype=jnp.int32)
    local = jnp.sum(jnp.where(slots[:, :, None] == choice, ghosts.reshape(-1), 0), axis=2)
    near = peer * per + local
    rows = jnp.concatenate([near, tile_ids, degrees[:, None]], axis=1).astype(bf16)
    flat = rows.reshape(-1)
    lanes = -(-flat.size // (width * size)) * size
    return jnp.pad(flat, (0, width * lanes - flat.size)).reshape(width, lanes)


def read_meta(raw, per, width_k, tile_count):
    sources = raw.shape[0]
    span = 2 * width_k + 1
    rows = raw.reshape(sources, -1)[:, : per * span].astype(jnp.int32).reshape(sources * per, span)
    near, tile, degrees = rows[:, :width_k], rows[:, width_k : 2 * width_k], rows[:, 2 * width_k]
    count = sources * per
    live = lax.broadcasted_iota(jnp.int32, near.shape, 1) < degrees[:, None]
    order = lax.broadcasted_iota(jnp.int32, near.shape, 0)
    empty = tile_count * count
    return {
        "near": near,
        "tile": tile,
        "live": live,
        "per": per,
        "weight": lax.rsqrt(degrees.astype(f32)),
        "near_flat": near.reshape(-1),
        "pick": jnp.where(live, tile * count + near, empty).reshape(-1),
        "pick_back": jnp.where(live, tile * count + order, empty).reshape(-1),
        "trips": (degrees + unroll - 1) // unroll,
    }


def swap(values, axis, bit):
    size = lax.axis_size(axis)
    return lax.ppermute(values, axis, [(i, i ^ bit) for i in range(size)])


def gather_rows(values, axis):
    size = lax.axis_size(axis)
    me = lax.axis_index(axis)
    held = values[None]
    bit = size // 2
    while bit:
        other = swap(held, axis, bit)
        upper = (me // bit) % 2 == 1
        held = jnp.concatenate(
            [jnp.where(upper, other, held)[:, None], jnp.where(upper, held, other)[:, None]], 1
        ).reshape((-1,) + values.shape)
        bit //= 2
    return held.reshape((-1,) + values.shape[1:])


def halve(parts, axis, bit, fraction):
    me = lax.axis_index(axis)
    mine = (me // bit) % 2
    lead = parts.shape[0]
    split = parts.reshape((2, lead // 2) + parts.shape[1:])
    keep = lax.dynamic_index_in_dim(split, mine, 0, keepdims=False)
    give = lax.dynamic_index_in_dim(split, 1 - mine, 0, keepdims=False)
    return keep + swap(give.astype(bf16), axis, bit).astype(f32)


def reduce_grad(left, right):
    feat_count, node_count = lax.axis_size("feat"), lax.axis_size("nodes")
    wide = right.shape[0] // feat_count
    me = lax.axis_index("feat")
    tall = right.reshape(feat_count, wide, right.shape[1])
    order, bit = [0], 1
    while bit < feat_count:
        order = [o + bit for o in order] + order
        bit *= 2
    product = lambda ids: nt_dot(left, jnp.concatenate([tall[me ^ i] for i in ids], 0))
    odd, even = [o for o in order if o & 1], [o for o in order if not o & 1]
    given = product(odd).astype(bf16)
    total = product(even) + swap(given, "feat", 1).astype(f32)
    bit = 2
    ids = even
    while bit < feat_count:
        far = [i for i, o in enumerate(ids) if o & bit]
        close = [i for i, o in enumerate(ids) if not o & bit]
        cols = lambda sel: jnp.concatenate([total[:, i * wide : (i + 1) * wide] for i in sel], 1)
        total = cols(close) + swap(cols(far).astype(bf16), "feat", bit).astype(f32)
        ids = [ids[i] for i in close]
        bit *= 2
    parts = total.reshape(node_count, -1, wide)
    parts = parts.reshape(node_count // 2, 2, -1, wide).transpose(1, 0, 2, 3).reshape(node_count, -1, wide)
    parts = halve(parts, "nodes", 1, 2)
    bit = node_count // 2
    while bit > 1:
        parts = halve(parts, "nodes", bit, 2)
        bit //= 2
    return parts.reshape(-1, wide)


def on_device(
    features, ghosts, slots, tile_ids, degrees, tile_table, weight_one, weight_two, cotangent
):
    node_count, feat_count = lax.axis_size("nodes"), lax.axis_size("feat")
    every = ("feat", "nodes")
    per, width_k = slots.shape
    size = tile_table.shape[1]
    rows = features.shape[0]
    width = features.shape[1] // node_count
    swap_all = lambda v, axes: lax.all_to_all(v, axes, split_axis=0, concat_axis=0, tiled=True)

    meta_block = pack_meta(ghosts, slots, tile_ids, degrees, width, size)
    sent = features.T.reshape(node_count, width, rows)
    sent = jnp.concatenate([sent, jnp.broadcast_to(meta_block, (node_count,) + meta_block.shape)], axis=2)
    feat_t = swap_all(sent, "nodes")
    cot_t = swap_all(cotangent.T.reshape(node_count, width, rows), "nodes")
    meta = read_meta(feat_t[:, :, rows:], per, width_k, tile_table.shape[0])

    first = gather_rows(weight_one.T, "feat")
    second = gather_rows(weight_two.T, "feat")

    def over_all(v):
        flat = v.reshape((feat_count * node_count,) + v.shape[2:])
        return swap_all(flat, every)

    agg = over_all(local_spread(feat_t, "N", "R", meta, tile_table, feat_count)).reshape(-1, rows // feat_count)
    back = over_all(local_spread(cot_t, "N", "R", meta, tile_table, feat_count, True)).reshape(-1, rows // feat_count)

    pre = jnp.dot(first, agg, preferred_element_type=f32)
    hidden = jax.nn.silu(pre).astype(bf16)
    wide_out = jnp.dot(second, hidden, preferred_element_type=f32).astype(bf16)
    out_t = swap_all(wide_out.reshape(feat_count * node_count, width, rows // feat_count), every)
    out_t = out_t.reshape(feat_count, node_count, width, rows // feat_count)
    out_n = swap_all(local_spread(out_t, "R", "N", meta, tile_table, feat_count), "nodes")
    output = out_n.reshape(-1, rows).T

    back_hidden = lax.dot_general(second, back, (((0,), (0,)), ((), ())), preferred_element_type=f32)
    sigma = jax.nn.sigmoid(pre)
    back_pre = (back_hidden * sigma * (1.0 + pre * (1.0 - sigma))).astype(bf16)
    grad_two = reduce_grad(hidden, back)
    grad_one = reduce_grad(agg, back_pre)
    return (output, grad_one, grad_two)


def solution(mesh):
    return jax.shard_map(
        on_device,
        mesh=mesh,
        in_specs=(
            P("nodes", "feat"),
            P("nodes", None),
            P("nodes", None),
            P("nodes", None),
            P("nodes"),
            P(),
            P(None, "feat"),
            P(None, "feat"),
            P("nodes", "feat"),
        ),
        out_specs=(P("nodes", "feat"), P("nodes", "feat"), P("nodes", "feat")),
        check_vma=False,
    )
```

```python
import functools

import jax
import jax.numpy as jnp
from jax import lax
from jax.experimental import pallas as pl
from jax.experimental.pallas import tpu as pltpu
from jax.sharding import PartitionSpec as P

unroll = 4
meta_rows = 16
bf16, f32 = jnp.bfloat16, jnp.float32
vmem = pl.BlockSpec(memory_space=pltpu.VMEM)
smem = pl.BlockSpec(memory_space=pltpu.SMEM)


def nt_dot(a, b):
    return lax.dot_general(a, b, (((1,), (1,)), ((), ())), preferred_element_type=f32)


def call(body, outs, in_specs, args, scratch=(), flops=0, out_specs=None):
    return pl.pallas_call(
        body,
        out_shape=[jax.ShapeDtypeStruct(s, d) for s, d in outs],
        in_specs=in_specs,
        out_specs=out_specs or [vmem] * len(outs),
        scratch_shapes=list(scratch),
        compiler_params=pltpu.CompilerParams(vmem_limit_bytes=48 * 1024 * 1024),
        cost_estimate=pl.CostEstimate(flops=flops, bytes_accessed=4 << 20, transcendentals=0),
    )(*args)


def meta_tile(ghost_at, degree_at, slots, tile_ids, owners, held, size):
    per, width_k = slots.shape
    near = jnp.zeros((per, width_k), jnp.int32)
    for s in range(owners * held):
        near = jnp.where(slots == s, (s // held) * per + ghost_at(s // held, s % held), near)
    row = lax.broadcasted_iota(jnp.int32, (per, size), 0)
    lane = lax.broadcasted_iota(jnp.int32, (per, size), 1)
    degree = jnp.zeros((per, size), jnp.int32)
    for r in range(per):
        degree = jnp.where(row == r, degree_at(r), degree)
    widen = lambda v: jnp.concatenate([v, jnp.zeros((per, size - width_k), jnp.int32)], axis=1)
    top = jnp.where(lane == width_k, degree, widen(near))
    return jnp.concatenate([top, widen(tile_ids)], axis=0).astype(f32).astype(bf16)


def pack_kernel(owners, held, ghosts, degrees, slots_ref, tiles_ref, feat_ref, cot_ref, o_ref):
    nodes, rows, size = o_ref.shape
    width = feat_ref.shape[1] // nodes
    per = feat_ref.shape[0] // size
    for which, ref in enumerate((feat_ref, cot_ref)):
        for b in range(per):
            turned = ref[b * size : (b + 1) * size, :].T
            first = (which * per + b) * width
            for n in range(nodes):
                o_ref[n, first : first + width, :] = turned[n * width : (n + 1) * width]
    tile = meta_tile(
        lambda p, c: ghosts[p, c], lambda r: degrees[r], slots_ref[...], tiles_ref[...], owners, held, size
    )
    for n in range(nodes):
        o_ref[n, rows - meta_rows :, :] = tile


def pack(features, cotangent, ghosts, slots, tile_ids, degrees, nodes, size):
    owners, held = ghosts.shape
    per = slots.shape[0]
    width = features.shape[1] // nodes
    if width % 16:
        turn = lambda v: v.reshape(per, size, nodes, width).transpose(2, 0, 3, 1).reshape(nodes, per * width, size)
        tile = meta_tile(lambda p, c: ghosts[p, c], lambda r: degrees[r], slots, tile_ids, owners, held, size)
        tile = jnp.broadcast_to(tile, (nodes,) + tile.shape)
        return jnp.concatenate([turn(features), turn(cotangent), tile], axis=1)
    shape = (nodes, 2 * per * width + meta_rows, size)
    return call(
        functools.partial(pack_kernel, owners, held),
        [(shape, bf16)],
        [smem, smem, vmem, vmem, vmem, vmem],
        (ghosts, degrees, slots, tile_ids, features, cotangent),
    )[0]


def form_products(left_at, count, width, tiles_ref, p_ref, transposed):
    tile_count, size = tiles_ref.shape[0], tiles_ref.shape[1]

    def pair(turn, carry):
        two = tiles_ref[pl.ds(2 * turn, 2)]
        if transposed:
            right = jnp.concatenate([two[0], two[1]], axis=1)
        else:
            right = two.reshape(2 * size, size)
        for first, left in left_at():
            res = jnp.dot(left, right, preferred_element_type=f32) if transposed else nt_dot(left, right)
            group = left.shape[0] // width
            for half in range(2):
                part = res[:, half * size : (half + 1) * size].reshape(group, width, size)
                p_ref[pl.ds((2 * turn + half) * count + first, group)] = part
        return carry

    lax.fori_loop(0, tile_count // 2, pair, 0)
    p_ref[tile_count * count] = jnp.zeros((width, size), f32)


def sum_entries(pick, near, r, width_k, p_ref):
    def chunk(c, acc):
        base = c * unroll
        terms = [p_ref[pick[r, base + u]] for u in range(unroll)]
        return acc + ((terms[0] + terms[1]) + (terms[2] + terms[3]))

    trips = (near[r, width_k] + (unroll - 1)) // unroll
    return lax.fori_loop(0, trips, chunk, jnp.zeros(p_ref.shape[1:], f32))


def first_kernel(per, width_k, v_ref, tiles_ref, o_ref, ids_ref, weight_ref, pick, pick_back, near, p_ref, sem, *sums):
    nodes, _, size = v_ref.shape
    width = o_ref.shape[2]
    share = o_ref.shape[3] // size
    count = nodes * per
    span = per * width
    empty = tiles_ref.shape[0] * count
    lane = lax.broadcasted_iota(jnp.int32, (per, size), 1)
    row = lax.broadcasted_iota(jnp.int32, (per, size), 0)
    for n in range(nodes):
        raw = v_ref[n, 2 * span :, :].astype(f32).astype(jnp.int32)
        links, tile = raw[:per], raw[per:]
        degree = jnp.broadcast_to(links[:, width_k : width_k + 1], (per, size))
        live = lane < degree
        block = slice(n * per, (n + 1) * per)
        ids_ref[0, block] = jnp.where(live, tile * count + links, empty)
        ids_ref[1, block] = jnp.where(live, tile * count + (row + n * per), empty)
        ids_ref[2, block] = links
        weight_ref[block] = lax.rsqrt(degree.astype(f32))
    copies = [pltpu.make_async_copy(ids_ref.at[i], ref, sem.at[i]) for i, ref in enumerate((pick, pick_back, near))]
    for copy in copies:
        copy.start()

    def lefts(first_row):
        def at():
            for n in range(0, nodes, 2):
                yield n * per, v_ref[n : n + 2, first_row : first_row + span, :].reshape(2 * span, size)

        return at

    form_products(lefts(0), count, width, tiles_ref, p_ref, False)
    for copy in copies:
        copy.wait()

    def forward_rows(n, carry):
        for b in range(per):
            r = n * per + b
            acc = sum_entries(pick, near, r, width_k, p_ref)
            own = v_ref[n, b * width : (b + 1) * width, :].astype(f32)
            j = b % share
            value = (own + weight_ref[pl.ds(r, 1), :] * acc).astype(bf16)
            o_ref[(b // share) * nodes + n, 0, :, j * size : (j + 1) * size] = value
        return carry

    lax.fori_loop(0, nodes, forward_rows, 0)

    form_products(lefts(span), count, width, tiles_ref, p_ref, True)
    for n in range(nodes):
        sums[0][n * per : (n + 1) * per] = v_ref[n, span : 2 * span, :].astype(f32).reshape(per, width, size)
    for total in sums[1:]:
        total[...] = jnp.zeros(total.shape, f32)

    def entry_row(r, carry):
        scale = weight_ref[pl.ds(r, 1), :]

        def chunk(c, inner):
            base = c * unroll
            for u in range(unroll):
                g = near[r, base + u]
                sums[u][g] = sums[u][g] + scale * p_ref[pick_back[r, base + u]]
            return inner

        return lax.fori_loop(0, (near[r, width_k] + (unroll - 1)) // unroll, chunk, carry)

    lax.fori_loop(0, count, entry_row, 0)

    def back_rows(n, carry):
        for b in range(per):
            r = n * per + b
            j = b % share
            value = ((sums[0][r] + sums[1][r]) + (sums[2][r] + sums[3][r])).astype(bf16)
            o_ref[(b // share) * nodes + n, 1, :, j * size : (j + 1) * size] = value
        return carry

    lax.fori_loop(0, nodes, back_rows, 0)


def last_kernel(per, width_k, pick, near, weight_ref, v_ref, tiles_ref, o_ref, x_ref, p_ref):
    nodes = o_ref.shape[0]
    count, width, size = x_ref.shape
    share = v_ref.shape[2] // size
    for f in range(per // share):
        for n in range(nodes):
            for j in range(share):
                x_ref[n * per + f * share + j] = v_ref[f * nodes + n, :, j * size : (j + 1) * size]

    def lefts():
        group = 512 // width
        for first in range(0, count, group):
            yield first, x_ref[first : first + group].reshape(group * width, size)

    form_products(lefts, count, width, tiles_ref, p_ref, False)

    def rows(n, carry):
        for b in range(per):
            r = n * per + b
            acc = sum_entries(pick, near, r, width_k, p_ref)
            value = x_ref[r].astype(f32) + weight_ref[pl.ds(r, 1), :] * acc
            o_ref[n, :, b * size : (b + 1) * size] = value.astype(bf16)
        return carry

    lax.fori_loop(0, nodes, rows, 0)


def plain_spread(x, ids, tiles, transposed):
    near, tile_ids, degrees = ids
    rows = jnp.arange(x.shape[0])
    kind = "gfi,tij->tgfj" if transposed else "gfj,tij->tgfi"
    products = jnp.einsum(kind, x, tiles, preferred_element_type=f32)
    weight = lax.rsqrt(degrees.astype(f32))

    def step(k, acc):
        g, t = near[:, k], tile_ids[:, k]
        scale = jnp.where(k < degrees, weight, 0.0)[:, None, None]
        if transposed:
            return acc.at[g].add(scale * products[t, rows])
        return acc + scale * products[t, g]

    return lax.fori_loop(0, near.shape[1], step, x.astype(f32)).astype(bf16)


def spread_first(v, tiles, per, width_k, feat_count):
    nodes, rows, size = v.shape
    width = (rows - meta_rows) // (2 * per)
    count, share = nodes * per, per // feat_count
    if width % 16:
        raw = v[:, rows - meta_rows :, :].astype(jnp.int32)
        links = raw[:, :per].reshape(count, size)
        ids = (links[:, :width_k], raw[:, per:].reshape(count, size)[:, :width_k], links[:, width_k])
        both = v[:, : rows - meta_rows].reshape(nodes, 2, per, width, size).transpose(1, 0, 2, 3, 4)
        both = both.reshape(2, count, width, size)
        out = jnp.stack([plain_spread(both[0], ids, tiles, False), plain_spread(both[1], ids, tiles, True)])
        out = out.reshape(2, nodes, feat_count, share, width, size).transpose(2, 1, 0, 4, 3, 5)
        return out.reshape(feat_count * nodes, 2, width, share * size), ids
    scratch = [pltpu.SMEM((count, size), jnp.int32)] * 3
    scratch += [pltpu.VMEM((tiles.shape[0] * count + 1, width, size), f32), pltpu.SemaphoreType.DMA((3,))]
    scratch += [pltpu.VMEM((count, width, size), f32)] * unroll
    out, ids, weight = call(
        functools.partial(first_kernel, per, width_k),
        [
            ((feat_count * nodes, 2, width, share * size), bf16),
            ((3, count, size), jnp.int32),
            ((count, size), f32),
        ],
        [vmem, vmem],
        (v, tiles),
        scratch,
        4 * tiles.shape[0] * count * width * size * size,
    )
    return out, (ids[0], ids[2], weight)


def spread_last(v, ids, tiles, per, width_k, nodes):
    size = tiles.shape[1]
    every, width, held = v.shape
    feat_count, share, count = every // nodes, held // size, nodes * per
    if width % 16:
        x = v.reshape(feat_count, nodes, width, share, size).transpose(1, 0, 3, 2, 4).reshape(count, width, size)
        out = plain_spread(x, ids, tiles, False)
        return out.reshape(nodes, per, width, size).transpose(0, 2, 1, 3).reshape(nodes, width, per * size)
    pick, near, weight = ids
    return call(
        functools.partial(last_kernel, per, width_k),
        [((nodes, width, per * size), bf16)],
        [smem, smem, vmem, vmem, vmem],
        (pick, near, weight, v, tiles),
        [
            pltpu.VMEM((count, width, size), bf16),
            pltpu.VMEM((tiles.shape[0] * count + 1, width, size), f32),
        ],
        2 * tiles.shape[0] * count * width * size * size,
    )[0]


def swap(values, axis, mask):
    return lax.ppermute(values, axis, [(i, i ^ mask) for i in range(lax.axis_size(axis))])


def gather_parts(values, axis):
    parts, offsets = [values], [0]
    bit = lax.axis_size(axis) // 2
    while bit:
        parts = parts + [swap(v, axis, bit) for v in parts]
        offsets = offsets + [o ^ bit for o in offsets]
        bit //= 2
    return parts, offsets


def project_kernel(offsets, *refs):
    count = len(offsets)
    v_ref, weights = refs[0], refs[1 : 1 + count]
    pre_ref, hidden_ref, y_ref, agg_ref = refs[1 + count : 5 + count]
    backs = refs[5 + count :]
    me = lax.axis_index("feat")
    wide = weights[0].shape[1]
    chunks, _, height, rows = v_ref.shape
    agg_ref[...] = v_ref[:, 0].reshape(chunks * height, rows)
    agg = agg_ref[...]
    place = [pl.ds(pl.multiple_of((me ^ o) * wide, wide), wide) for o in offsets]
    for at, w_ref in zip(place, weights):
        pre = jnp.dot(w_ref[0], agg, preferred_element_type=f32)
        pre_ref[at, :] = pre
        hidden_ref[at, :] = (pre * jax.nn.sigmoid(pre)).astype(bf16)
    hidden = hidden_ref[...]
    for at, w_ref in zip(place, weights):
        y_ref[at, :] = jnp.dot(w_ref[1], hidden, preferred_element_type=f32).astype(bf16)
    split = chunks // count
    for o, b_ref in zip(offsets, backs):
        if split:
            b_ref[...] = v_ref[pl.ds((me ^ o) * split, split), 1].reshape(wide, rows)
        else:
            b_ref[...] = v_ref[0, 1, pl.ds(pl.multiple_of((me ^ o) * wide, wide), wide), :]


def back_kernel(offsets, *refs):
    count = len(offsets)
    pre_ref, weights, backs, outs = refs[0], refs[1 : 1 + count], refs[1 + count : 1 + 2 * count], refs[1 + 2 * count :]
    me = lax.axis_index("feat")
    wide = weights[0].shape[1]
    for o, o_ref in zip(offsets, outs):
        at = pl.ds(pl.multiple_of((me ^ o) * wide, wide), wide)
        total = None
        for w_ref, b_ref in zip(weights, backs):
            term = lax.dot_general(
                w_ref[1, :, at], b_ref[...], (((0,), (0,)), ((), ())), preferred_element_type=f32
            )
            total = term if total is None else total + term
        pre = pre_ref[at, :]
        sigma = jax.nn.sigmoid(pre)
        o_ref[...] = (total * sigma * (1.0 + pre * (1.0 - sigma))).astype(bf16)


def grad_kernel(count, *refs):
    lefts, rights, give_ref, keep_ref = refs[:count], refs[count : 2 * count], refs[2 * count], refs[2 * count + 1]
    side = lax.axis_index("nodes") % 2
    half, tall, _ = keep_ref.shape
    for h in range(half):
        for mine in (False, True):
            row = (2 * h + (side if mine else 1 - side)) * tall
            at = pl.ds(pl.multiple_of(row, tall), tall)
            total = None
            for left, right in zip(lefts, rights):
                term = nt_dot(left[at, :], right[...])
                total = term if total is None else total + term
            if mine:
                keep_ref[h] = total
            else:
                give_ref[h] = total.astype(bf16)


def split_kernel(keep_ref, came_ref, mine_ref, *outs):
    me = lax.axis_index("nodes") // 2
    mine_ref[...] = keep_ref[me] + came_ref[me].astype(f32)
    for i, o_ref in enumerate(outs):
        to = me ^ (i + 1)
        o_ref[...] = (keep_ref[to] + came_ref[to].astype(f32)).astype(bf16)


def weight_grad(lefts, rights):
    nodes = lax.axis_size("nodes")
    count = len(lefts)
    half, tall, wide = nodes // 2, lefts[0].shape[0] // nodes, rights[0].shape[0]
    flops = 2 * count * lefts[0].shape[0] * lefts[0].shape[1] * wide
    give, keep = call(
        functools.partial(grad_kernel, count),
        [((half, tall, wide), bf16), ((half, tall, wide), f32)],
        [vmem] * (2 * count),
        (*lefts, *rights),
        flops=flops,
    )
    came = swap(give, "nodes", 1)
    mine, *rest = call(
        split_kernel,
        [((tall, wide), f32)] + [((tall, wide), bf16)] * (half - 1),
        [vmem] * 2,
        (keep, came),
    )
    for i, part in enumerate(rest):
        mine = mine + swap(part, "nodes", 2 * (i + 1)).astype(f32)
    return mine


def on_device(
    features, ghosts, slots, tile_ids, degrees, tile_table, weight_one, weight_two, cotangent
):
    nodes, feat_count = lax.axis_size("nodes"), lax.axis_size("feat")
    every = ("feat", "nodes")
    per, width_k = slots.shape
    size = tile_table.shape[1]
    rows, wide = features.shape
    held = rows // feat_count
    hidden_width = wide * feat_count
    exchange = lambda v, axes: lax.all_to_all(v, axes, split_axis=0, concat_axis=0, tiled=True)

    sent = pack(features, cotangent, ghosts, slots, tile_ids, degrees, nodes, size)
    came = exchange(sent, "nodes")
    weights, offsets = gather_parts(jnp.stack([weight_one.T, weight_two.T]), "feat")
    spreads, ids = spread_first(came, tile_table, per, width_k, feat_count)
    gathered = exchange(spreads, every)
    if gathered.shape[2] % 16:
        gathered = gathered.transpose(1, 0, 2, 3).reshape(1, 2, hidden_width, held)

    parts = len(offsets)
    pre, hidden, wide_out, agg, *backs = call(
        functools.partial(project_kernel, offsets),
        [((hidden_width, held), f32)] + [((hidden_width, held), bf16)] * 3 + [((wide, held), bf16)] * parts,
        [vmem] * (1 + parts),
        (gathered, *weights),
        flops=4 * hidden_width * hidden_width * held,
    )
    out_t = exchange(wide_out.reshape(feat_count * nodes, wide // nodes, held), every)

    turn = lambda blocks: [blocks[0]] + [swap(b, "feat", o) for b, o in zip(blocks[1:], offsets[1:])]
    hidden_parts, _ = gather_parts(hidden, "feat")
    grad_two = weight_grad(hidden_parts, turn(backs))
    agg_parts, _ = gather_parts(agg, "feat")
    back_pre = call(
        functools.partial(back_kernel, offsets),
        [((wide, held), bf16)] * parts,
        [vmem] * (1 + 2 * parts),
        (pre, *weights, *backs),
        flops=2 * hidden_width * hidden_width * held,
    )
    grad_one = weight_grad(agg_parts, turn(back_pre))

    out_n = exchange(spread_last(out_t, ids, tile_table, per, width_k, nodes), "nodes")
    output = out_n.reshape(wide, rows).T
    return (output, grad_one, grad_two)


def solution(mesh):
    return jax.shard_map(
        on_device,
        mesh=mesh,
        in_specs=(
            P("nodes", "feat"),
            P("nodes", None),
            P("nodes", None),
            P("nodes", None),
            P("nodes"),
            P(),
            P(None, "feat"),
            P(None, "feat"),
            P("nodes", "feat"),
        ),
        out_specs=(P("nodes", "feat"), P("nodes", "feat"), P("nodes", "feat")),
        check_vma=False,
    )
```

```python
import functools

import jax
import jax.numpy as jnp
from jax import lax
from jax.experimental import pallas as pl
from jax.experimental.pallas import tpu as pltpu
from jax.sharding import PartitionSpec as P

unroll = 4
tile_step = 4
meta_rows = 16
bf16, f32 = jnp.bfloat16, jnp.float32
vmem = pl.BlockSpec(memory_space=pltpu.VMEM)
smem = pl.BlockSpec(memory_space=pltpu.SMEM)


def nt_dot(a, b):
    return lax.dot_general(a, b, (((1,), (1,)), ((), ())), preferred_element_type=f32)


def call(body, outs, in_specs, args, scratch=(), flops=0, limit=56):
    return pl.pallas_call(
        body,
        out_shape=[jax.ShapeDtypeStruct(s, d) for s, d in outs],
        in_specs=in_specs,
        out_specs=[vmem] * len(outs),
        scratch_shapes=list(scratch),
        compiler_params=pltpu.CompilerParams(vmem_limit_bytes=limit * 1024 * 1024),
        cost_estimate=pl.CostEstimate(flops=flops, bytes_accessed=4 << 20, transcendentals=0),
    )(*args)


def meta_tile(ghost_at, degree_at, slots, tile_ids, owners, held, size):
    per, width_k = slots.shape
    near = jnp.zeros((per, width_k), jnp.int32)
    for s in range(owners * held):
        near = jnp.where(slots == s, (s // held) * per + ghost_at(s // held, s % held), near)
    row = lax.broadcasted_iota(jnp.int32, (per, size), 0)
    lane = lax.broadcasted_iota(jnp.int32, (per, size), 1)
    degree = jnp.zeros((per, size), jnp.int32)
    for r in range(per):
        degree = jnp.where(row == r, degree_at(r), degree)
    widen = lambda v: jnp.concatenate([v, jnp.zeros((per, size - width_k), jnp.int32)], axis=1)
    top = jnp.where(lane == width_k, degree, widen(near))
    return jnp.concatenate([top, widen(tile_ids)], axis=0).astype(f32).astype(bf16)


def pack_kernel(owners, held, ghosts, degrees, slots_ref, tiles_ref, feat_ref, o_ref):
    nodes, rows, size = o_ref.shape
    width = feat_ref.shape[1] // nodes
    per = feat_ref.shape[0] // size
    for b in range(per):
        turned = feat_ref[b * size : (b + 1) * size, :].T
        for n in range(nodes):
            o_ref[n, b * width : (b + 1) * width, :] = turned[n * width : (n + 1) * width]
    tile = meta_tile(
        lambda p, c: ghosts[p, c], lambda r: degrees[r], slots_ref[...], tiles_ref[...], owners, held, size
    )
    for n in range(nodes):
        o_ref[n, rows - meta_rows :, :] = tile


def turn_blocks(values, nodes, size):
    per, width = values.shape[0] // size, values.shape[1] // nodes
    return values.reshape(per, size, nodes, width).transpose(2, 0, 3, 1).reshape(nodes, per * width, size)


def pack(features, ghosts, slots, tile_ids, degrees, nodes, size):
    owners, held = ghosts.shape
    per = slots.shape[0]
    width = features.shape[1] // nodes
    if width % 16:
        tile = meta_tile(lambda p, c: ghosts[p, c], lambda r: degrees[r], slots, tile_ids, owners, held, size)
        tile = jnp.broadcast_to(tile, (nodes,) + tile.shape)
        return jnp.concatenate([turn_blocks(features, nodes, size), tile], axis=1)
    return call(
        functools.partial(pack_kernel, owners, held),
        [((nodes, per * width + meta_rows, size), bf16)],
        [smem, smem, vmem, vmem, vmem],
        (ghosts, degrees, slots, tile_ids, features),
    )[0]


def turn_kernel(v_ref, *refs):
    outs, turned_ref = refs[:-1], refs[-1]
    size = outs[0].shape[1]
    per = v_ref.shape[0] // size
    width = v_ref.shape[1] // len(outs)
    me = lax.axis_index("nodes")
    for b in range(per):
        turned_ref[b] = v_ref[b * size : (b + 1) * size, :].T
    for i, o_ref in enumerate(outs):
        at = pl.ds(pl.multiple_of((me ^ i) * width, width), width)
        for b in range(per):
            o_ref[b * width : (b + 1) * width, :] = turned_ref[b, at, :]


def pack_parts(values, nodes, size):
    per, width = values.shape[0] // size, values.shape[1] // nodes
    if width % 16:
        me = lax.axis_index("nodes")
        turned = turn_blocks(values, nodes, size)
        return [lax.dynamic_index_in_dim(turned, me ^ i, 0, keepdims=False) for i in range(nodes)]
    return call(
        turn_kernel,
        [((per * width, size), bf16)] * nodes,
        [vmem],
        (values,),
        [pltpu.VMEM((per, values.shape[1], size), bf16)],
    )


def form_products(lefts, count, width, tiles_ref, p_ref, transposed):
    tile_count, size = tiles_ref.shape[0], tiles_ref.shape[1]

    def step(turn, carry):
        some = tiles_ref[pl.ds(tile_step * turn, tile_step)]
        if transposed:
            right = jnp.concatenate([some[i] for i in range(tile_step)], axis=1)
        else:
            right = some.reshape(tile_step * size, size)
        for first, load in lefts:
            left = load()
            res = jnp.dot(left, right, preferred_element_type=f32) if transposed else nt_dot(left, right)
            group = left.shape[0] // width
            for i in range(tile_step):
                part = res[:, i * size : (i + 1) * size].reshape(group, width, size)
                p_ref[pl.ds((tile_step * turn + i) * count + first, group)] = part
        return carry

    lax.fori_loop(0, tile_count // tile_step, step, 0)
    p_ref[tile_count * count] = jnp.zeros((width, size), f32)


def sum_entries(pick, r, width_k, p_ref):
    terms = [p_ref[pick[r, k]] for k in range(width_k)]
    while len(terms) > 1:
        terms = [terms[i] + terms[i + 1] for i in range(0, len(terms) - 1, 2)] + terms[len(terms) & ~1 :]
    return terms[0]


def first_kernel(per, width_k, v_ref, tiles_ref, o_ref, ids_ref, weight_ref, pick, p_ref, sem):
    nodes, _, size = v_ref.shape
    width = o_ref.shape[1]
    share = o_ref.shape[2] // size
    count = nodes * per
    span = per * width
    empty = tiles_ref.shape[0] * count
    lane = lax.broadcasted_iota(jnp.int32, (per, size), 1)
    row = lax.broadcasted_iota(jnp.int32, (per, size), 0)
    for n in range(nodes):
        raw = v_ref[n, span:, :].astype(f32).astype(jnp.int32)
        links, tile = raw[:per], raw[per:]
        degree = jnp.broadcast_to(links[:, width_k : width_k + 1], (per, size))
        live = lane < degree
        block = slice(n * per, (n + 1) * per)
        ids_ref[0, block] = jnp.where(live, tile * count + links, empty)
        ids_ref[1, block] = jnp.where(live, tile * count + (row + n * per), empty)
        ids_ref[2, block] = links
        weight_ref[block] = lax.rsqrt(degree.astype(f32))
    copy = pltpu.make_async_copy(ids_ref.at[0], pick, sem)
    copy.start()
    lefts = [(n * per, lambda n=n: v_ref[n, :span, :]) for n in range(nodes)]
    form_products(lefts, count, width, tiles_ref, p_ref, False)
    copy.wait()

    def rows(n, carry):
        for b in range(per):
            r = n * per + b
            own = v_ref[n, b * width : (b + 1) * width, :].astype(f32)
            j = b % share
            value = (own + weight_ref[pl.ds(r, 1), :] * sum_entries(pick, r, width_k, p_ref)).astype(bf16)
            o_ref[(b // share) * nodes + n, :, j * size : (j + 1) * size] = value
        return carry

    lax.fori_loop(0, nodes, rows, 0)


def back_spread_kernel(per, width_k, nodes, pick, near, weight_ref, tiles_ref, *refs):
    parts, outs, p_ref, sums = refs[:nodes], refs[nodes : 2 * nodes], refs[2 * nodes], refs[2 * nodes + 1 :]
    me = lax.axis_index("nodes")
    size = tiles_ref.shape[1]
    width = outs[0].shape[0]
    count = nodes * per
    block = [pl.multiple_of((me ^ i) * per, per) for i in range(nodes)]
    form_products(
        [(block[i], lambda i=i: parts[i][...]) for i in range(nodes)], count, width, tiles_ref, p_ref, True
    )
    for i in range(nodes):
        sums[0][pl.ds(block[i], per)] = parts[i][...].astype(f32).reshape(per, width, size)
    for total in sums[1:]:
        total[...] = jnp.zeros(total.shape, f32)

    def entry_row(r, carry):
        scale = weight_ref[pl.ds(r, 1), :]

        def chunk(c, inner):
            base = c * unroll
            for u in range(unroll):
                g = near[r, base + u]
                sums[u][g] = sums[u][g] + scale * p_ref[pick[r, base + u]]
            return inner

        return lax.fori_loop(0, (near[r, width_k] + (unroll - 1)) // unroll, chunk, carry)

    lax.fori_loop(0, count, entry_row, 0)
    for i in range(nodes):
        for b in range(per):
            r = block[i] + b
            value = ((sums[0][r] + sums[1][r]) + (sums[2][r] + sums[3][r])).astype(bf16)
            outs[i][:, b * size : (b + 1) * size] = value


def last_kernel(per, width_k, pick, weight_ref, v_ref, tiles_ref, o_ref, x_ref, p_ref):
    nodes = o_ref.shape[0]
    count, width, size = x_ref.shape
    share = v_ref.shape[2] // size
    for f in range(per // share):
        for n in range(nodes):
            for j in range(share):
                x_ref[n * per + f * share + j] = v_ref[f * nodes + n, :, j * size : (j + 1) * size]
    group = 256 // width
    lefts = [
        (first, lambda first=first: x_ref[first : first + group].reshape(group * width, size))
        for first in range(0, count, group)
    ]
    form_products(lefts, count, width, tiles_ref, p_ref, False)

    def rows(n, carry):
        for b in range(per):
            r = n * per + b
            acc = sum_entries(pick, r, width_k, p_ref)
            value = x_ref[r].astype(f32) + weight_ref[pl.ds(r, 1), :] * acc
            o_ref[n, :, b * size : (b + 1) * size] = value.astype(bf16)
        return carry

    lax.fori_loop(0, nodes, rows, 0)


def plain_spread(x, ids, tiles, transposed):
    near, tile_ids, degrees = ids
    rows = jnp.arange(x.shape[0])
    kind = "gfi,tij->tgfj" if transposed else "gfj,tij->tgfi"
    products = jnp.einsum(kind, x, tiles, preferred_element_type=f32)
    weight = lax.rsqrt(degrees.astype(f32))

    def step(k, acc):
        g, t = near[:, k], tile_ids[:, k]
        scale = jnp.where(k < degrees, weight, 0.0)[:, None, None]
        if transposed:
            return acc.at[g].add(scale * products[t, rows])
        return acc + scale * products[t, g]

    return lax.fori_loop(0, near.shape[1], step, x.astype(f32)).astype(bf16)


def product_flops(tiles, count, width):
    return 2 * tiles.shape[0] * count * width * tiles.shape[1] * tiles.shape[1]


def product_scratch(tiles, count, width):
    return pltpu.VMEM((tiles.shape[0] * count + 1, width, tiles.shape[1]), f32)


def spread_first(v, tiles, per, width_k, feat_count):
    nodes, rows, size = v.shape
    width = (rows - meta_rows) // per
    count, share = nodes * per, per // feat_count
    if width % 16:
        raw = v[:, rows - meta_rows :, :].astype(jnp.int32)
        links = raw[:, :per].reshape(count, size)
        ids = (links[:, :width_k], raw[:, per:].reshape(count, size)[:, :width_k], links[:, width_k])
        out = plain_spread(v[:, : rows - meta_rows].reshape(count, width, size), ids, tiles, False)
        out = out.reshape(nodes, feat_count, share, width, size).transpose(1, 0, 3, 2, 4)
        return out.reshape(feat_count * nodes, width, share * size), ids
    return_ids = ((3, count, size), jnp.int32)
    out, ids, weight = call(
        functools.partial(first_kernel, per, width_k),
        [((feat_count * nodes, width, share * size), bf16), return_ids, ((count, size), f32)],
        [vmem, vmem],
        (v, tiles),
        [
            pltpu.SMEM((count, size), jnp.int32),
            product_scratch(tiles, count, width),
            pltpu.SemaphoreType.DMA,
        ],
        product_flops(tiles, count, width),
    )
    return out, (ids[0], ids[1], ids[2], weight)


def spread_back(parts, ids, tiles, per, width_k):
    nodes, size = len(parts), tiles.shape[1]
    width, count = parts[0].shape[0] // per, len(parts) * per
    if width % 16:
        me = lax.axis_index("nodes")
        order = me ^ jnp.arange(nodes)
        x = jnp.stack(parts)[order].reshape(count, width, size)
        out = plain_spread(x, ids, tiles, True)
        out = out.reshape(nodes, per, width, size).transpose(0, 2, 1, 3).reshape(nodes, width, per * size)[order]
        return [out[i] for i in range(nodes)]
    _, pick_back, near, weight = ids
    return call(
        functools.partial(back_spread_kernel, per, width_k, nodes),
        [((width, per * size), bf16)] * nodes,
        [smem, smem, vmem, vmem] + [vmem] * nodes,
        (pick_back, near, weight, tiles, *parts),
        [product_scratch(tiles, count, width)] + [pltpu.VMEM((count, width, size), f32)] * unroll,
        product_flops(tiles, count, width),
    )


def spread_last(v, ids, tiles, per, width_k, nodes):
    size = tiles.shape[1]
    every, width, held = v.shape
    feat_count, share, count = every // nodes, held // size, nodes * per
    if width % 16:
        x = v.reshape(feat_count, nodes, width, share, size).transpose(1, 0, 3, 2, 4).reshape(count, width, size)
        out = plain_spread(x, ids, tiles, False)
        return out.reshape(nodes, per, width, size).transpose(0, 2, 1, 3).reshape(nodes, width, per * size)
    pick, _, _, weight = ids
    return call(
        functools.partial(last_kernel, per, width_k),
        [((nodes, width, per * size), bf16)],
        [smem, vmem, vmem, vmem],
        (pick, weight, v, tiles),
        [pltpu.VMEM((count, width, size), bf16), product_scratch(tiles, count, width)],
        product_flops(tiles, count, width),
    )[0]


def swap(values, axis, mask):
    return lax.ppermute(values, axis, [(i, i ^ mask) for i in range(lax.axis_size(axis))])


def gather_parts(values, axis):
    parts, offsets = [values], [0]
    bit = lax.axis_size(axis) // 2
    while bit:
        parts = parts + [swap(v, axis, bit) for v in parts]
        offsets = offsets + [o ^ bit for o in offsets]
        bit //= 2
    return parts, offsets


def join_kernel(nodes, offsets, *refs):
    parts, outs = refs[:nodes], refs[nodes:]
    me_n, me_f = lax.axis_index("nodes"), lax.axis_index("feat")
    width = parts[0].shape[0]
    held = outs[0].shape[1]
    for o, o_ref in zip(offsets, outs):
        cols = pl.ds(pl.multiple_of((me_f ^ o) * held, held), held)
        for i, part in enumerate(parts):
            o_ref[pl.ds(pl.multiple_of((me_n ^ i) * width, width), width), :] = part[:, cols]


def join_parts(parts, offsets, held):
    nodes, width = len(parts), parts[0].shape[0]
    if width % 16:
        whole = jnp.stack(parts)[lax.axis_index("nodes") ^ jnp.arange(nodes)].reshape(nodes * width, -1)
        first = lax.axis_index("feat")
        return [lax.dynamic_slice_in_dim(whole, (first ^ o) * held, held, 1) for o in offsets]
    return call(
        functools.partial(join_kernel, nodes, offsets),
        [((nodes * width, held), bf16)] * len(offsets),
        [vmem] * nodes,
        parts,
    )


def project_kernel(offsets, agg_ref, *refs):
    count = len(offsets)
    weights, (pre_ref, hidden_ref, y_ref) = refs[:count], refs[count:]
    me = lax.axis_index("feat")
    wide = weights[0].shape[1]
    agg = agg_ref[...]
    place = [pl.ds(pl.multiple_of((me ^ o) * wide, wide), wide) for o in offsets]
    for at, w_ref in zip(place, weights):
        pre = jnp.dot(w_ref[0], agg, preferred_element_type=f32)
        pre_ref[at, :] = pre
        hidden_ref[at, :] = (pre * jax.nn.sigmoid(pre)).astype(bf16)
    hidden = hidden_ref[...]
    for at, w_ref in zip(place, weights):
        y_ref[at, :] = jnp.dot(w_ref[1], hidden, preferred_element_type=f32).astype(bf16)


def back_kernel(offsets, *refs):
    count = len(offsets)
    pre_ref, weights, backs, outs = refs[0], refs[1 : 1 + count], refs[1 + count : 1 + 2 * count], refs[1 + 2 * count :]
    me = lax.axis_index("feat")
    wide = weights[0].shape[1]
    for o, o_ref in zip(offsets, outs):
        at = pl.ds(pl.multiple_of((me ^ o) * wide, wide), wide)
        total = None
        for w_ref, b_ref in zip(weights, backs):
            term = lax.dot_general(
                w_ref[1, :, at], b_ref[...], (((0,), (0,)), ((), ())), preferred_element_type=f32
            )
            total = term if total is None else total + term
        pre = pre_ref[at, :]
        sigma = jax.nn.sigmoid(pre)
        o_ref[...] = (total * sigma * (1.0 + pre * (1.0 - sigma))).astype(bf16)


def grad_kernel(count, *refs):
    lefts, rights, give_ref, keep_ref = refs[:count], refs[count : 2 * count], refs[2 * count], refs[2 * count + 1]
    side = lax.axis_index("nodes") % 2
    half, tall, _ = keep_ref.shape
    for h in range(half):
        for mine in (False, True):
            row = (2 * h + (side if mine else 1 - side)) * tall
            at = pl.ds(pl.multiple_of(row, tall), tall)
            total = None
            for left, right in zip(lefts, rights):
                term = nt_dot(left[at, :], right[...])
                total = term if total is None else total + term
            if mine:
                keep_ref[h] = total
            else:
                give_ref[h] = total.astype(bf16)


def split_kernel(keep_ref, came_ref, mine_ref, *outs):
    me = lax.axis_index("nodes") // 2
    mine_ref[...] = keep_ref[me] + came_ref[me].astype(f32)
    for i, o_ref in enumerate(outs):
        to = me ^ (i + 1)
        o_ref[...] = (keep_ref[to] + came_ref[to].astype(f32)).astype(bf16)


def weight_grad(lefts, rights):
    nodes = lax.axis_size("nodes")
    count = len(lefts)
    half, tall, wide = nodes // 2, lefts[0].shape[0] // nodes, rights[0].shape[0]
    flops = 2 * count * lefts[0].shape[0] * lefts[0].shape[1] * wide
    give, keep = call(
        functools.partial(grad_kernel, count),
        [((half, tall, wide), bf16), ((half, tall, wide), f32)],
        [vmem] * (2 * count),
        (*lefts, *rights),
        flops=flops,
    )
    came = swap(give, "nodes", 1)
    mine, *rest = call(
        split_kernel,
        [((tall, wide), f32)] + [((tall, wide), bf16)] * (half - 1),
        [vmem] * 2,
        (keep, came),
    )
    for i, part in enumerate(rest):
        mine = mine + swap(part, "nodes", 2 * (i + 1)).astype(f32)
    return mine


def on_device(
    features, ghosts, slots, tile_ids, degrees, tile_table, weight_one, weight_two, cotangent
):
    nodes, feat_count = lax.axis_size("nodes"), lax.axis_size("feat")
    every = ("feat", "nodes")
    per, width_k = slots.shape
    size = tile_table.shape[1]
    rows, wide = features.shape
    held = rows // feat_count
    hidden_width = wide * feat_count
    exchange = lambda v, axes: lax.all_to_all(v, axes, split_axis=0, concat_axis=0, tiled=True)

    sent = pack(features, ghosts, slots, tile_ids, degrees, nodes, size)
    came = exchange(sent, "nodes")
    weights, offsets = gather_parts(jnp.stack([weight_one.T, weight_two.T]), "feat")
    around = lambda parts: [parts[0]] + [swap(p, "nodes", i) for i, p in enumerate(parts) if i]
    turn = lambda blocks: [blocks[0]] + [swap(b, "feat", o) for b, o in zip(blocks[1:], offsets[1:])]
    cot_parts = around(pack_parts(cotangent, nodes, size))

    spread, ids = spread_first(came, tile_table, per, width_k, feat_count)
    agg = exchange(spread, every).reshape(hidden_width, held)
    rights = join_parts(around(spread_back(cot_parts, ids, tile_table, per, width_k)), offsets, held)
    backs = turn(rights)

    parts = len(offsets)
    pre, hidden, wide_out = call(
        functools.partial(project_kernel, offsets),
        [((hidden_width, held), f32)] + [((hidden_width, held), bf16)] * 2,
        [vmem] * (1 + parts),
        (agg, *weights),
        flops=4 * hidden_width * hidden_width * held,
    )
    out_t = exchange(wide_out.reshape(feat_count * nodes, wide // nodes, held), every)

    hidden_parts, _ = gather_parts(hidden, "feat")
    grad_two = weight_grad(hidden_parts, rights)
    agg_parts, _ = gather_parts(agg, "feat")
    back_pre = call(
        functools.partial(back_kernel, offsets),
        [((wide, held), bf16)] * parts,
        [vmem] * (1 + 2 * parts),
        (pre, *weights, *backs),
        flops=2 * hidden_width * hidden_width * held,
    )
    grad_one = weight_grad(agg_parts, turn(back_pre))

    out_n = exchange(spread_last(out_t, ids, tile_table, per, width_k, nodes), "nodes")
    output = out_n.reshape(wide, rows).T
    return (output, grad_one, grad_two)


def solution(mesh):
    return jax.shard_map(
        on_device,
        mesh=mesh,
        in_specs=(
            P("nodes", "feat"),
            P("nodes", None),
            P("nodes", None),
            P("nodes", None),
            P("nodes"),
            P(),
            P(None, "feat"),
            P(None, "feat"),
            P("nodes", "feat"),
        ),
        out_specs=(P("nodes", "feat"), P("nodes", "feat"), P("nodes", "feat")),
        check_vma=False,
    )
```

```python
import functools

import jax
import jax.numpy as jnp
from jax import lax
from jax.experimental import pallas as pl
from jax.experimental.pallas import tpu as pltpu
from jax.sharding import PartitionSpec as P

unroll = 4
tile_step = 4
meta_rows = 16
bf16, f32 = jnp.bfloat16, jnp.float32
vmem = pl.BlockSpec(memory_space=pltpu.VMEM)
smem = pl.BlockSpec(memory_space=pltpu.SMEM)


def nt_dot(a, b):
    return lax.dot_general(a, b, (((1,), (1,)), ((), ())), preferred_element_type=f32)


def call(body, outs, in_specs, args, scratch=(), flops=0, limit=16, moved=0):
    return pl.pallas_call(
        body,
        out_shape=[jax.ShapeDtypeStruct(s, d) for s, d in outs],
        in_specs=in_specs,
        out_specs=[vmem] * len(outs),
        scratch_shapes=list(scratch),
        compiler_params=pltpu.CompilerParams(vmem_limit_bytes=limit * 1024 * 1024),
        cost_estimate=pl.CostEstimate(flops=flops, bytes_accessed=moved, transcendentals=0),
    )(*args)


def after(values, *earlier):
    return lax.optimization_barrier((values, earlier))[0]


def meta_tile(ghost_at, degree_at, slots, tile_ids, owners, held, size):
    per, width_k = slots.shape
    near = jnp.zeros((per, width_k), jnp.int32)
    for s in range(owners * held):
        near = jnp.where(slots == s, (s // held) * per + ghost_at(s // held, s % held), near)
    row = lax.broadcasted_iota(jnp.int32, (per, size), 0)
    lane = lax.broadcasted_iota(jnp.int32, (per, size), 1)
    degree = jnp.zeros((per, size), jnp.int32)
    for r in range(per):
        degree = jnp.where(row == r, degree_at(r), degree)
    widen = lambda v: jnp.concatenate([v, jnp.zeros((per, size - width_k), jnp.int32)], axis=1)
    top = jnp.where(lane == width_k, degree, widen(near))
    return jnp.concatenate([top, widen(tile_ids)], axis=0).astype(f32).astype(bf16)


def pack_kernel(owners, held, ghosts, degrees, slots_ref, tiles_ref, feat_ref, o_ref):
    nodes, rows, size = o_ref.shape
    width = feat_ref.shape[1] // nodes
    per = feat_ref.shape[0] // size
    for b in range(per):
        turned = feat_ref[b * size : (b + 1) * size, :].T
        for n in range(nodes):
            o_ref[n, b * width : (b + 1) * width, :] = turned[n * width : (n + 1) * width]
    tile = meta_tile(
        lambda p, c: ghosts[p, c], lambda r: degrees[r], slots_ref[...], tiles_ref[...], owners, held, size
    )
    for n in range(nodes):
        o_ref[n, rows - meta_rows :, :] = tile


def turn_blocks(values, nodes, size):
    per, width = values.shape[0] // size, values.shape[1] // nodes
    return values.reshape(per, size, nodes, width).transpose(2, 0, 3, 1).reshape(nodes, per * width, size)


def pack(features, ghosts, slots, tile_ids, degrees, nodes, size):
    owners, held = ghosts.shape
    per = slots.shape[0]
    width = features.shape[1] // nodes
    if width % 16:
        tile = meta_tile(lambda p, c: ghosts[p, c], lambda r: degrees[r], slots, tile_ids, owners, held, size)
        tile = jnp.broadcast_to(tile, (nodes,) + tile.shape)
        return jnp.concatenate([turn_blocks(features, nodes, size), tile], axis=1)
    return call(
        functools.partial(pack_kernel, owners, held),
        [((nodes, per * width + meta_rows, size), bf16)],
        [smem, smem, vmem, vmem, vmem],
        (ghosts, degrees, slots, tile_ids, features),
    )[0]


def turn_kernel(v_ref, *refs):
    outs, turned_ref = refs[:-1], refs[-1]
    size = outs[0].shape[1]
    per = v_ref.shape[0] // size
    width = v_ref.shape[1] // len(outs)
    me = lax.axis_index("nodes")
    for b in range(per):
        turned_ref[b] = v_ref[b * size : (b + 1) * size, :].T
    for i, o_ref in enumerate(outs):
        at = pl.ds(pl.multiple_of((me ^ i) * width, width), width)
        for b in range(per):
            o_ref[b * width : (b + 1) * width, :] = turned_ref[b, at, :]


def pack_parts(values, nodes, size):
    per, width = values.shape[0] // size, values.shape[1] // nodes
    if width % 16:
        me = lax.axis_index("nodes")
        turned = turn_blocks(values, nodes, size)
        return [lax.dynamic_index_in_dim(turned, me ^ i, 0, keepdims=False) for i in range(nodes)]
    return call(
        turn_kernel,
        [((per * width, size), bf16)] * nodes,
        [vmem],
        (values,),
        [pltpu.VMEM((per, values.shape[1], size), bf16)],
    )


def form_products(lefts, count, width, tiles_ref, p_ref, transposed):
    tile_count, size = tiles_ref.shape[0], tiles_ref.shape[1]

    def step(turn, carry):
        some = tiles_ref[pl.ds(tile_step * turn, tile_step)]
        if transposed:
            right = jnp.concatenate([some[i] for i in range(tile_step)], axis=1)
        else:
            right = some.reshape(tile_step * size, size)
        for first, load in lefts:
            left = load()
            res = jnp.dot(left, right, preferred_element_type=f32) if transposed else nt_dot(left, right)
            group = left.shape[0] // width
            for i in range(tile_step):
                part = res[:, i * size : (i + 1) * size].reshape(group, width, size)
                p_ref[pl.ds((tile_step * turn + i) * count + first, group)] = part
        return carry

    lax.fori_loop(0, tile_count // tile_step, step, 0)
    p_ref[tile_count * count] = jnp.zeros((width, size), f32)


def sum_entries(pick, r, width_k, p_ref):
    terms = [p_ref[pick[r, k]] for k in range(width_k)]
    while len(terms) > 1:
        terms = [terms[i] + terms[i + 1] for i in range(0, len(terms) - 1, 2)] + terms[len(terms) & ~1 :]
    return terms[0]


def first_kernel(per, width_k, v_ref, tiles_ref, o_ref, ids_ref, weight_ref, pick, p_ref, sem):
    nodes, _, size = v_ref.shape
    width = o_ref.shape[1]
    share = o_ref.shape[2] // size
    count = nodes * per
    span = per * width
    empty = tiles_ref.shape[0] * count
    lane = lax.broadcasted_iota(jnp.int32, (per, size), 1)
    row = lax.broadcasted_iota(jnp.int32, (per, size), 0)
    for n in range(nodes):
        raw = v_ref[n, span:, :].astype(f32).astype(jnp.int32)
        links, tile = raw[:per], raw[per:]
        degree = jnp.broadcast_to(links[:, width_k : width_k + 1], (per, size))
        live = lane < degree
        block = slice(n * per, (n + 1) * per)
        ids_ref[0, block] = jnp.where(live, tile * count + links, empty)
        ids_ref[1, block] = jnp.where(live, tile * count + (row + n * per), empty)
        ids_ref[2, block] = links
        weight_ref[block] = lax.rsqrt(degree.astype(f32))
    copy = pltpu.make_async_copy(ids_ref.at[0], pick, sem)
    copy.start()
    lefts = [(n * per, lambda n=n: v_ref[n, :span, :]) for n in range(nodes)]
    form_products(lefts, count, width, tiles_ref, p_ref, False)
    copy.wait()

    def rows(n, carry):
        for b in range(per):
            r = n * per + b
            own = v_ref[n, b * width : (b + 1) * width, :].astype(f32)
            j = b % share
            value = (own + weight_ref[pl.ds(r, 1), :] * sum_entries(pick, r, width_k, p_ref)).astype(bf16)
            o_ref[(b // share) * nodes + n, :, j * size : (j + 1) * size] = value
        return carry

    lax.fori_loop(0, nodes, rows, 0)


def back_spread_kernel(per, width_k, nodes, pick, near, weight_ref, tiles_ref, *refs):
    parts, o_ref, p_ref, sums = refs[:nodes], refs[nodes], refs[nodes + 1], refs[nodes + 2 :]
    me = lax.axis_index("nodes")
    size = tiles_ref.shape[1]
    width = o_ref.shape[1]
    share = o_ref.shape[2] // size
    count = nodes * per
    block = [pl.multiple_of((me ^ i) * per, per) for i in range(nodes)]
    form_products(
        [(block[i], lambda i=i: parts[i][...]) for i in range(nodes)], count, width, tiles_ref, p_ref, True
    )
    for i in range(nodes):
        sums[0][pl.ds(block[i], per)] = parts[i][...].astype(f32).reshape(per, width, size)
    for total in sums[1:]:
        total[...] = jnp.zeros(total.shape, f32)

    def entry_row(r, carry):
        scale = weight_ref[pl.ds(r, 1), :]

        def chunk(c, inner):
            base = c * unroll
            for u in range(unroll):
                g = near[r, base + u]
                sums[u][g] = sums[u][g] + scale * p_ref[pick[r, base + u]]
            return inner

        return lax.fori_loop(0, (near[r, width_k] + (unroll - 1)) // unroll, chunk, carry)

    lax.fori_loop(0, count, entry_row, 0)

    def rows(n, carry):
        for b in range(per):
            r = n * per + b
            j = b % share
            value = ((sums[0][r] + sums[1][r]) + (sums[2][r] + sums[3][r])).astype(bf16)
            o_ref[(b // share) * nodes + n, :, j * size : (j + 1) * size] = value
        return carry

    lax.fori_loop(0, nodes, rows, 0)


def last_kernel(per, width_k, pick, weight_ref, v_ref, tiles_ref, o_ref, x_ref, p_ref):
    nodes = o_ref.shape[0]
    count, width, size = x_ref.shape
    share = v_ref.shape[2] // size
    for f in range(per // share):
        for n in range(nodes):
            for j in range(share):
                x_ref[n * per + f * share + j] = v_ref[f * nodes + n, :, j * size : (j + 1) * size]
    group = 256 // width
    lefts = [
        (first, lambda first=first: x_ref[first : first + group].reshape(group * width, size))
        for first in range(0, count, group)
    ]
    form_products(lefts, count, width, tiles_ref, p_ref, False)

    def rows(n, carry):
        for b in range(per):
            r = n * per + b
            acc = sum_entries(pick, r, width_k, p_ref)
            value = x_ref[r].astype(f32) + weight_ref[pl.ds(r, 1), :] * acc
            o_ref[n, :, b * size : (b + 1) * size] = value.astype(bf16)
        return carry

    lax.fori_loop(0, nodes, rows, 0)


def plain_spread(x, ids, tiles, transposed):
    near, tile_ids, degrees = ids
    rows = jnp.arange(x.shape[0])
    kind = "gfi,tij->tgfj" if transposed else "gfj,tij->tgfi"
    products = jnp.einsum(kind, x, tiles, preferred_element_type=f32)
    weight = lax.rsqrt(degrees.astype(f32))

    def step(k, acc):
        g, t = near[:, k], tile_ids[:, k]
        scale = jnp.where(k < degrees, weight, 0.0)[:, None, None]
        if transposed:
            return acc.at[g].add(scale * products[t, rows])
        return acc + scale * products[t, g]

    return lax.fori_loop(0, near.shape[1], step, x.astype(f32)).astype(bf16)


def product_flops(tiles, count, width):
    return 2 * tiles.shape[0] * count * width * tiles.shape[1] * tiles.shape[1]


def product_scratch(tiles, count, width):
    return pltpu.VMEM((tiles.shape[0] * count + 1, width, tiles.shape[1]), f32)


def spread_first(v, tiles, per, width_k, feat_count):
    nodes, rows, size = v.shape
    width = (rows - meta_rows) // per
    count, share = nodes * per, per // feat_count
    if width % 16:
        raw = v[:, rows - meta_rows :, :].astype(jnp.int32)
        links = raw[:, :per].reshape(count, size)
        ids = (links[:, :width_k], raw[:, per:].reshape(count, size)[:, :width_k], links[:, width_k])
        out = plain_spread(v[:, : rows - meta_rows].reshape(count, width, size), ids, tiles, False)
        out = out.reshape(nodes, feat_count, share, width, size).transpose(1, 0, 3, 2, 4)
        return out.reshape(feat_count * nodes, width, share * size), ids
    return_ids = ((3, count, size), jnp.int32)
    out, ids, weight = call(
        functools.partial(first_kernel, per, width_k),
        [((feat_count * nodes, width, share * size), bf16), return_ids, ((count, size), f32)],
        [vmem, vmem],
        (v, tiles),
        [
            pltpu.SMEM((count, size), jnp.int32),
            product_scratch(tiles, count, width),
            pltpu.SemaphoreType.DMA,
        ],
        0,
        28,
    )
    return out, (ids[0], ids[1], ids[2], weight)


def spread_back(parts, ids, tiles, per, width_k, feat_count):
    nodes, size = len(parts), tiles.shape[1]
    width, count, share = parts[0].shape[0] // per, len(parts) * per, per // feat_count
    if width % 16:
        order = lax.axis_index("nodes") ^ jnp.arange(nodes)
        out = plain_spread(jnp.stack(parts)[order].reshape(count, width, size), ids, tiles, True)
        out = out.reshape(nodes, feat_count, share, width, size).transpose(1, 0, 3, 2, 4)
        return out.reshape(feat_count * nodes, width, share * size)
    _, pick_back, near, weight = ids
    return call(
        functools.partial(back_spread_kernel, per, width_k, nodes),
        [((feat_count * nodes, width, share * size), bf16)],
        [smem, smem, vmem, vmem] + [vmem] * nodes,
        (pick_back, near, weight, tiles, *parts),
        [product_scratch(tiles, count, width)] + [pltpu.VMEM((count, width, size), f32)] * unroll,
        product_flops(tiles, count, width),
        28,
        4 << 20,
    )[0]


def spread_last(v, ids, tiles, per, width_k, nodes):
    size = tiles.shape[1]
    every, width, held = v.shape
    feat_count, share, count = every // nodes, held // size, nodes * per
    if width % 16:
        x = v.reshape(feat_count, nodes, width, share, size).transpose(1, 0, 3, 2, 4).reshape(count, width, size)
        out = plain_spread(x, ids, tiles, False)
        return out.reshape(nodes, per, width, size).transpose(0, 2, 1, 3).reshape(nodes, width, per * size)
    pick, _, _, weight = ids
    return call(
        functools.partial(last_kernel, per, width_k),
        [((nodes, width, per * size), bf16)],
        [smem, vmem, vmem, vmem],
        (pick, weight, v, tiles),
        [pltpu.VMEM((count, width, size), bf16), product_scratch(tiles, count, width)],
        0,
        28,
    )[0]


def swap(values, axis, mask):
    return lax.ppermute(values, axis, [(i, i ^ mask) for i in range(lax.axis_size(axis))])


def gather_parts(values, axis):
    parts, offsets = [values], [0]
    bit = lax.axis_size(axis) // 2
    while bit:
        parts = parts + [swap(v, axis, bit) for v in parts]
        offsets = offsets + [o ^ bit for o in offsets]
        bit //= 2
    return parts, offsets


def project_kernel(offsets, agg_ref, *refs):
    count = len(offsets)
    weights, (pre_ref, hidden_ref, y_ref) = refs[:count], refs[count:]
    me = lax.axis_index("feat")
    wide = weights[0].shape[1]
    agg = agg_ref[...]
    place = [pl.ds(pl.multiple_of((me ^ o) * wide, wide), wide) for o in offsets]
    for at, w_ref in zip(place, weights):
        pre = jnp.dot(w_ref[0], agg, preferred_element_type=f32)
        pre_ref[at, :] = pre
        hidden_ref[at, :] = (pre * jax.nn.sigmoid(pre)).astype(bf16)
    hidden = hidden_ref[...]
    for at, w_ref in zip(place, weights):
        y_ref[at, :] = jnp.dot(w_ref[1], hidden, preferred_element_type=f32).astype(bf16)


def halves_of(left_ref, right_ref, give_ref, keep_ref, offsets):
    me = lax.axis_index("feat")
    nodes, tall, wide = give_ref.shape[1:]
    left = left_ref[...]
    for i, o in enumerate(offsets):
        for out, to in ((give_ref, me ^ o ^ 1), (keep_ref, me ^ o)):
            right = right_ref[pl.ds(pl.multiple_of(to * wide, wide), wide), :]
            out[i] = nt_dot(left, right).reshape(nodes, tall, wide).astype(out.dtype)


def product_kernel(offsets, left_ref, right_ref, give_ref, keep_ref):
    halves_of(left_ref, right_ref, give_ref, keep_ref, offsets)


def back_kernel(offsets, evens, pre_ref, back_ref, left_ref, *refs):
    count = len(offsets)
    weights, (give_ref, keep_ref, out_ref) = refs[:count], refs[count:]
    me = lax.axis_index("feat")
    wide = weights[0].shape[1]
    place = [pl.ds(pl.multiple_of((me ^ o) * wide, wide), wide) for o in offsets]
    for at in place:
        total = None
        for w_ref, rows in zip(weights, place):
            term = lax.dot_general(
                w_ref[1, :, at], back_ref[rows, :], (((0,), (0,)), ((), ())), preferred_element_type=f32
            )
            total = term if total is None else total + term
        pre = pre_ref[at, :]
        sigma = jax.nn.sigmoid(pre)
        out_ref[at, :] = (total * sigma * (1.0 + pre * (1.0 - sigma))).astype(bf16)
    halves_of(left_ref, out_ref, give_ref, keep_ref, evens)


def quarter_kernel(keep_ref, came_ref, mine_ref, *outs):
    side = lax.axis_index("nodes") % 2
    half = mine_ref.shape[0]
    spots = [(i, b) for i in range(keep_ref.shape[0]) for b in range(2)]
    for (i, b), o_ref in zip(spots, (mine_ref,) + outs):
        for h in range(half):
            row = 2 * h + (side ^ b)
            o_ref[h] = (keep_ref[i, row] + came_ref[i, row].astype(f32)).astype(o_ref.dtype)


def split_kernel(keep_ref, *refs):
    half = keep_ref.shape[0]
    came, mine_ref, outs = refs[:-half], refs[-half], refs[len(refs) - half + 1 :]
    me = lax.axis_index("nodes") // 2
    for i, o_ref in enumerate((mine_ref,) + outs):
        total = keep_ref[me ^ i]
        for ref in came:
            total = total + ref[me ^ i].astype(f32)
        o_ref[...] = total.astype(o_ref.dtype)


def even_offsets():
    return list(range(0, lax.axis_size("feat"), 2))


def grad_shapes(left, right):
    nodes, count = lax.axis_size("nodes"), lax.axis_size("feat")
    shape = (count // 2, nodes, left.shape[0] // nodes, right.shape[0] // count)
    return [(shape, bf16), (shape, f32)]


def quarters(swapped, keep):
    _, nodes, tall, wide = keep.shape
    evens, feat_count = even_offsets(), lax.axis_size("feat")
    spots = [(o, b) for o in evens for b in range(2)][1:]
    shape = (nodes // 2, tall, wide)
    mine, *rest = call(
        quarter_kernel,
        [(shape, f32)] + [(shape, bf16)] * len(spots),
        [vmem] * 2,
        (keep, swapped),
    )
    ring = range(nodes * feat_count)
    moved = [
        lax.ppermute(v, ("nodes", "feat"), [(i, i ^ (b * feat_count + o)) for i in ring]) for v, (o, b) in zip(rest, spots)
    ]
    return mine, *moved


def grad_sum(keep, *came):
    half, tall, wide = keep.shape
    mine, *rest = call(
        split_kernel,
        [((tall, wide), f32)] + [((tall, wide), bf16)] * (half - 1),
        [vmem] * (1 + len(came)),
        (keep, *came),
    )
    for i, part in enumerate(rest):
        mine = mine + swap(part, "nodes", 2 * (i + 1)).astype(f32)
    return mine


def on_device(
    features, ghosts, slots, tile_ids, degrees, tile_table, weight_one, weight_two, cotangent
):
    nodes, feat_count = lax.axis_size("nodes"), lax.axis_size("feat")
    every = ("feat", "nodes")
    per, width_k = slots.shape
    size = tile_table.shape[1]
    rows, wide = features.shape
    held = rows // feat_count
    hidden_width = wide * feat_count
    exchange = lambda v, axes: lax.all_to_all(v, axes, split_axis=0, concat_axis=0, tiled=True)

    sent = pack(features, ghosts, slots, tile_ids, degrees, nodes, size)
    came = exchange(sent, "nodes")
    packed = pack_parts(after(cotangent, sent), nodes, size)
    first, second = after((weight_one, weight_two), sent)
    weights, offsets = gather_parts(jnp.stack([first.T, second.T]), "feat")

    spread, ids = spread_first(after(came, packed), tile_table, per, width_k, feat_count)
    cot_parts = [packed[0]] + [swap(p, "nodes", i) for i, p in enumerate(packed) if i]
    agg = exchange(after(spread, *cot_parts), every).reshape(hidden_width, held)
    back = spread_back(cot_parts, ids, tile_table, per, width_k, feat_count)
    agg = after(agg, back)
    back = exchange(back, every).reshape(hidden_width, held)

    parts = len(offsets)
    pre, hidden, wide_out = call(
        functools.partial(project_kernel, offsets),
        [((hidden_width, held), f32)] + [((hidden_width, held), bf16)] * 2,
        [vmem] * (1 + parts),
        (agg, *weights),
        flops=4 * hidden_width * hidden_width * held,
        moved=4 << 20,
    )
    wide_out = after(wide_out, back)
    out_t = exchange(wide_out.reshape(feat_count * nodes, wide // nodes, held), every)

    evens = even_offsets()
    flops = 2 * hidden_width * hidden_width * held
    give_two, keep_two = call(
        functools.partial(product_kernel, evens), grad_shapes(hidden, back), [vmem] * 2, (hidden, back), flops=flops, moved=4 << 20
    )
    swapped_two = swap(give_two, "feat", 1)
    give_one, keep_one, _ = call(
        functools.partial(back_kernel, offsets, evens),
        grad_shapes(agg, back) + [((hidden_width, held), bf16)],
        [vmem] * (3 + parts),
        (pre, after(back, swapped_two), agg, *weights),
        flops=2 * flops,
        moved=4 << 20,
    )
    quarters_two = quarters(swapped_two, keep_two)
    quarters_one = quarters(swap(give_one, "feat", 1), keep_one)

    out_t = after(out_t, quarters_two[0])
    last = spread_last(out_t, ids, tile_table, per, width_k, nodes)
    out_n = exchange(after(last, *quarters_two), "nodes")
    grad_two = grad_sum(*after(quarters_two, last))
    grad_one = grad_sum(*after(quarters_one, last))
    output = out_n.reshape(wide, rows).T
    return (output, grad_one, grad_two)


def solution(mesh):
    return jax.shard_map(
        on_device,
        mesh=mesh,
        in_specs=(
            P("nodes", "feat"),
            P("nodes", None),
            P("nodes", None),
            P("nodes", None),
            P("nodes"),
            P(),
            P(None, "feat"),
            P(None, "feat"),
            P("nodes", "feat"),
        ),
        out_specs=(P("nodes", "feat"), P("nodes", "feat"), P("nodes", "feat")),
        check_vma=False,
    )
```

```python
import functools

import jax
import jax.numpy as jnp
from jax import lax
from jax.experimental import pallas as pl
from jax.experimental.pallas import tpu as pltpu
from jax.sharding import PartitionSpec as P

unroll = 4
tile_step = 4
meta_rows = 16
bf16, f32 = jnp.bfloat16, jnp.float32
vmem = pl.BlockSpec(memory_space=pltpu.VMEM)
smem = pl.BlockSpec(memory_space=pltpu.SMEM)
far = object()


def nt_dot(a, b):
    return lax.dot_general(a, b, (((1,), (1,)), ((), ())), preferred_element_type=f32)


def call(body, outs, in_specs, args, scratch=(), flops=0, limit=16, moved=0, sent=()):
    return pl.pallas_call(
        body,
        out_shape=[(pltpu.HBM if i in sent else jax.ShapeDtypeStruct)(s, d) for i, (s, d) in enumerate(outs)],
        in_specs=[vmem if spec is far else spec for spec in in_specs],
        out_specs=[vmem] * len(outs),
        scratch_shapes=list(scratch),
        compiler_params=pltpu.CompilerParams(vmem_limit_bytes=limit * 1024 * 1024),
        cost_estimate=pl.CostEstimate(flops=flops, bytes_accessed=moved, transcendentals=0),
    )(*[v for v in args])


def after(values, *earlier):
    return lax.optimization_barrier((values, earlier))[0]


def meta_tile(ghost_at, degree_at, slots, tile_ids, owners, held, size):
    per, width_k = slots.shape
    near = jnp.zeros((per, width_k), jnp.int32)
    for s in range(owners * held):
        near = jnp.where(slots == s, (s // held) * per + ghost_at(s // held, s % held), near)
    row = lax.broadcasted_iota(jnp.int32, (per, size), 0)
    lane = lax.broadcasted_iota(jnp.int32, (per, size), 1)
    degree = jnp.zeros((per, size), jnp.int32)
    for r in range(per):
        degree = jnp.where(row == r, degree_at(r), degree)
    widen = lambda v: jnp.concatenate([v, jnp.zeros((per, size - width_k), jnp.int32)], axis=1)
    top = jnp.where(lane == width_k, degree, widen(near))
    return jnp.concatenate([top, widen(tile_ids)], axis=0).astype(f32).astype(bf16)


def pack_kernel(owners, held, ghosts, degrees, slots_ref, tiles_ref, feat_ref, o_ref):
    nodes, rows, size = o_ref.shape
    width = feat_ref.shape[1] // nodes
    per = feat_ref.shape[0] // size
    for b in range(per):
        turned = feat_ref[b * size : (b + 1) * size, :].T
        for n in range(nodes):
            o_ref[n, b * width : (b + 1) * width, :] = turned[n * width : (n + 1) * width]
    tile = meta_tile(
        lambda p, c: ghosts[p : p + 1, c : c + 1], lambda r: degrees[r], slots_ref[...], tiles_ref[...], owners, held, size
    )
    for n in range(nodes):
        o_ref[n, rows - meta_rows :, :] = tile


def turn_blocks(values, nodes, size):
    per, width = values.shape[0] // size, values.shape[1] // nodes
    return values.reshape(per, size, nodes, width).transpose(2, 0, 3, 1).reshape(nodes, per * width, size)


def pack(features, ghosts, slots, tile_ids, degrees, nodes, size):
    owners, held = ghosts.shape
    per = slots.shape[0]
    width = features.shape[1] // nodes
    if width % 16:
        tile = meta_tile(lambda p, c: ghosts[p, c], lambda r: degrees[r], slots, tile_ids, owners, held, size)
        tile = jnp.broadcast_to(tile, (nodes,) + tile.shape)
        return jnp.concatenate([turn_blocks(features, nodes, size), tile], axis=1)
    return call(
        functools.partial(pack_kernel, owners, held),
        [((nodes, per * width + meta_rows, size), bf16)],
        [vmem, smem, vmem, vmem, vmem],
        (ghosts, degrees, slots, tile_ids, features),
        sent=(0,),
    )[0]


def turn_kernel(v_ref, *refs):
    outs, turned_ref = refs[:-1], refs[-1]
    size = outs[0].shape[1]
    per = v_ref.shape[0] // size
    width = v_ref.shape[1] // len(outs)
    me = lax.axis_index("nodes")
    for b in range(per):
        turned_ref[b] = v_ref[b * size : (b + 1) * size, :].T
    for i, o_ref in enumerate(outs):
        at = pl.ds(pl.multiple_of((me ^ i) * width, width), width)
        for b in range(per):
            o_ref[b * width : (b + 1) * width, :] = turned_ref[b, at, :]


def pack_parts(values, nodes, size):
    per, width = values.shape[0] // size, values.shape[1] // nodes
    if width % 16:
        me = lax.axis_index("nodes")
        turned = turn_blocks(values, nodes, size)
        return [lax.dynamic_index_in_dim(turned, me ^ i, 0, keepdims=False) for i in range(nodes)]
    return call(
        turn_kernel,
        [((per * width, size), bf16)] * nodes,
        [far],
        (values,),
        [pltpu.VMEM((per, values.shape[1], size), bf16)],
        sent=tuple(range(nodes)),
    )


def form_products(lefts, count, width, tiles_ref, p_ref, transposed):
    tile_count, size = tiles_ref.shape[0], tiles_ref.shape[1]

    def step(turn, carry):
        some = tiles_ref[pl.ds(tile_step * turn, tile_step)]
        if transposed:
            right = jnp.concatenate([some[i] for i in range(tile_step)], axis=1)
        else:
            right = some.reshape(tile_step * size, size)
        for first, load in lefts:
            left = load()
            res = jnp.dot(left, right, preferred_element_type=f32) if transposed else nt_dot(left, right)
            group = left.shape[0] // width
            for i in range(tile_step):
                part = res[:, i * size : (i + 1) * size].reshape(group, width, size)
                p_ref[pl.ds((tile_step * turn + i) * count + first, group)] = part
        return carry

    lax.fori_loop(0, tile_count // tile_step, step, 0)
    p_ref[tile_count * count] = jnp.zeros((width, size), f32)


def sum_entries(pick, r, width_k, p_ref):
    terms = [p_ref[pick[r, k]] for k in range(width_k)]
    while len(terms) > 1:
        terms = [terms[i] + terms[i + 1] for i in range(0, len(terms) - 1, 2)] + terms[len(terms) & ~1 :]
    return terms[0]


def first_kernel(per, width_k, v_ref, tiles_ref, o_ref, ids_ref, weight_ref, pick, p_ref, sem):
    nodes, _, size = v_ref.shape
    width = o_ref.shape[1]
    share = o_ref.shape[2] // size
    count = nodes * per
    span = per * width
    empty = tiles_ref.shape[0] * count
    lane = lax.broadcasted_iota(jnp.int32, (per, size), 1)
    row = lax.broadcasted_iota(jnp.int32, (per, size), 0)
    for n in range(nodes):
        raw = v_ref[n, span:, :].astype(f32).astype(jnp.int32)
        links, tile = raw[:per], raw[per:]
        degree = jnp.broadcast_to(links[:, width_k : width_k + 1], (per, size))
        live = lane < degree
        block = slice(n * per, (n + 1) * per)
        ids_ref[0, block] = jnp.where(live, tile * count + links, empty)
        ids_ref[1, block] = jnp.where(live, tile * count + (row + n * per), empty)
        ids_ref[2, block] = links
        weight_ref[block] = lax.rsqrt(degree.astype(f32))
    copy = pltpu.make_async_copy(ids_ref.at[0], pick, sem)
    copy.start()
    lefts = [(n * per, lambda n=n: v_ref[n, :span, :]) for n in range(nodes)]
    form_products(lefts, count, width, tiles_ref, p_ref, False)
    copy.wait()

    def rows(n, carry):
        for b in range(per):
            r = n * per + b
            own = v_ref[n, b * width : (b + 1) * width, :].astype(f32)
            j = b % share
            value = (own + weight_ref[pl.ds(r, 1), :] * sum_entries(pick, r, width_k, p_ref)).astype(bf16)
            o_ref[(b // share) * nodes + n, :, j * size : (j + 1) * size] = value
        return carry

    lax.fori_loop(0, nodes, rows, 0)


def back_spread_kernel(per, width_k, nodes, pick, near, weight_ref, tiles_ref, *refs):
    parts, o_ref, p_ref, sums = refs[:nodes], refs[nodes], refs[nodes + 1], refs[nodes + 2 :]
    me = lax.axis_index("nodes")
    size = tiles_ref.shape[1]
    width = o_ref.shape[1]
    share = o_ref.shape[2] // size
    count = nodes * per
    block = [pl.multiple_of((me ^ i) * per, per) for i in range(nodes)]
    form_products(
        [(block[i], lambda i=i: parts[i][...]) for i in range(nodes)], count, width, tiles_ref, p_ref, True
    )
    for i in range(nodes):
        sums[0][pl.ds(block[i], per)] = parts[i][...].astype(f32).reshape(per, width, size)
    for total in sums[1:]:
        total[...] = jnp.zeros(total.shape, f32)

    def entry_row(r, carry):
        scale = weight_ref[pl.ds(r, 1), :]

        def chunk(c, inner):
            base = c * unroll
            for u in range(unroll):
                g = near[r, base + u]
                sums[u][g] = sums[u][g] + scale * p_ref[pick[r, base + u]]
            return inner

        return lax.fori_loop(0, (near[r, width_k] + (unroll - 1)) // unroll, chunk, carry)

    lax.fori_loop(0, count, entry_row, 0)

    def rows(n, carry):
        for b in range(per):
            r = n * per + b
            j = b % share
            value = ((sums[0][r] + sums[1][r]) + (sums[2][r] + sums[3][r])).astype(bf16)
            o_ref[(b // share) * nodes + n, :, j * size : (j + 1) * size] = value
        return carry

    lax.fori_loop(0, nodes, rows, 0)


def last_kernel(per, width_k, pick, weight_ref, v_ref, tiles_ref, o_ref, x_ref, p_ref):
    nodes = o_ref.shape[0]
    count, width, size = x_ref.shape
    share = v_ref.shape[2] // size
    for f in range(per // share):
        for n in range(nodes):
            for j in range(share):
                x_ref[n * per + f * share + j] = v_ref[f * nodes + n, :, j * size : (j + 1) * size]
    group = 256 // width
    lefts = [
        (first, lambda first=first: x_ref[first : first + group].reshape(group * width, size))
        for first in range(0, count, group)
    ]
    form_products(lefts, count, width, tiles_ref, p_ref, False)

    def rows(n, carry):
        for b in range(per):
            r = n * per + b
            acc = sum_entries(pick, r, width_k, p_ref)
            value = x_ref[r].astype(f32) + weight_ref[pl.ds(r, 1), :] * acc
            o_ref[n, :, b * size : (b + 1) * size] = value.astype(bf16)
        return carry

    lax.fori_loop(0, nodes, rows, 0)


def plain_spread(x, ids, tiles, transposed):
    near, tile_ids, degrees = ids
    rows = jnp.arange(x.shape[0])
    kind = "gfi,tij->tgfj" if transposed else "gfj,tij->tgfi"
    products = jnp.einsum(kind, x, tiles, preferred_element_type=f32)
    weight = lax.rsqrt(degrees.astype(f32))

    def step(k, acc):
        g, t = near[:, k], tile_ids[:, k]
        scale = jnp.where(k < degrees, weight, 0.0)[:, None, None]
        if transposed:
            return acc.at[g].add(scale * products[t, rows])
        return acc + scale * products[t, g]

    return lax.fori_loop(0, near.shape[1], step, x.astype(f32)).astype(bf16)


def product_flops(tiles, count, width):
    return 2 * tiles.shape[0] * count * width * tiles.shape[1] * tiles.shape[1]


def product_scratch(tiles, count, width):
    return pltpu.VMEM((tiles.shape[0] * count + 1, width, tiles.shape[1]), f32)


def spread_first(v, tiles, per, width_k, feat_count):
    nodes, rows, size = v.shape
    width = (rows - meta_rows) // per
    count, share = nodes * per, per // feat_count
    if width % 16:
        raw = v[:, rows - meta_rows :, :].astype(jnp.int32)
        links = raw[:, :per].reshape(count, size)
        ids = (links[:, :width_k], raw[:, per:].reshape(count, size)[:, :width_k], links[:, width_k])
        out = plain_spread(v[:, : rows - meta_rows].reshape(count, width, size), ids, tiles, False)
        out = out.reshape(nodes, feat_count, share, width, size).transpose(1, 0, 3, 2, 4)
        return out.reshape(feat_count * nodes, width, share * size), ids
    return_ids = ((3, count, size), jnp.int32)
    out, ids, weight = call(
        functools.partial(first_kernel, per, width_k),
        [((feat_count * nodes, width, share * size), bf16), return_ids, ((count, size), f32)],
        [far, far],
        (v, tiles),
        [
            pltpu.SMEM((count, size), jnp.int32),
            product_scratch(tiles, count, width),
            pltpu.SemaphoreType.DMA,
        ],
        0,
        28,
        sent=(0,),
    )
    return out, (ids[0], ids[1], ids[2], weight)


def spread_back(parts, ids, tiles, per, width_k, feat_count):
    nodes, size = len(parts), tiles.shape[1]
    width, count, share = parts[0].shape[0] // per, len(parts) * per, per // feat_count
    if width % 16:
        order = lax.axis_index("nodes") ^ jnp.arange(nodes)
        out = plain_spread(jnp.stack(parts)[order].reshape(count, width, size), ids, tiles, True)
        out = out.reshape(nodes, feat_count, share, width, size).transpose(1, 0, 3, 2, 4)
        return out.reshape(feat_count * nodes, width, share * size)
    _, pick_back, near, weight = ids
    return call(
        functools.partial(back_spread_kernel, per, width_k, nodes),
        [((feat_count * nodes, width, share * size), bf16)],
        [smem, smem, vmem, far] + [far] * nodes,
        (pick_back, near, weight, tiles, *parts),
        [product_scratch(tiles, count, width)] + [pltpu.VMEM((count, width, size), f32)] * unroll,
        product_flops(tiles, count, width),
        28,
        4 << 20,
        (0,),
    )[0]


def spread_last(v, ids, tiles, per, width_k, nodes):
    size = tiles.shape[1]
    every, width, held = v.shape
    feat_count, share, count = every // nodes, held // size, nodes * per
    if width % 16:
        x = v.reshape(feat_count, nodes, width, share, size).transpose(1, 0, 3, 2, 4).reshape(count, width, size)
        out = plain_spread(x, ids, tiles, False)
        return out.reshape(nodes, per, width, size).transpose(0, 2, 1, 3).reshape(nodes, width, per * size)
    pick, _, _, weight = ids
    return call(
        functools.partial(last_kernel, per, width_k),
        [((nodes, width, per * size), bf16)],
        [smem, vmem, far, far],
        (pick, weight, v, tiles),
        [pltpu.VMEM((count, width, size), bf16), product_scratch(tiles, count, width)],
        10 * product_flops(tiles, count, width),
        28,
        sent=(0,),
    )[0]


def swap(values, axis, mask):
    return lax.ppermute(values, axis, [(i, i ^ mask) for i in range(lax.axis_size(axis))])


def gather_parts(values, axis):
    parts, offsets = [values], [0]
    bit = lax.axis_size(axis) // 2
    while bit:
        parts = parts + [swap(v, axis, bit) for v in parts]
        offsets = offsets + [o ^ bit for o in offsets]
        bit //= 2
    return parts, offsets


def project_kernel(offsets, agg_ref, *refs):
    count = len(offsets)
    weights, (pre_ref, hidden_ref, y_ref) = refs[:count], refs[count:]
    me = lax.axis_index("feat")
    wide = weights[0].shape[1]
    agg = agg_ref[...]
    place = [pl.ds(pl.multiple_of((me ^ o) * wide, wide), wide) for o in offsets]
    for at, w_ref in zip(place, weights):
        pre = jnp.dot(w_ref[0], agg, preferred_element_type=f32)
        pre_ref[at, :] = pre
        hidden_ref[at, :] = (pre * jax.nn.sigmoid(pre)).astype(bf16)
    hidden = hidden_ref[...]
    for at, w_ref in zip(place, weights):
        y_ref[at, :] = jnp.dot(w_ref[1], hidden, preferred_element_type=f32).astype(bf16)


def side_rows(left_ref, tall):
    side = lax.axis_index("nodes") % 2
    pick = lambda row: left_ref[pl.ds(pl.multiple_of(row * tall, tall), tall), :]
    half = left_ref.shape[0] // (2 * tall)
    return [jnp.concatenate([pick(2 * h + (side ^ b)) for h in range(half)], axis=0) for b in range(2)]


def give_blocks(left_ref, right_ref, outs, offsets):
    me = lax.axis_index("feat")
    half, tall, wide = outs[0].shape
    lefts = side_rows(left_ref, tall)
    for i, o in enumerate(offsets):
        right = right_ref[pl.ds(pl.multiple_of((me ^ o ^ 1) * wide, wide), wide), :]
        for b in range(2):
            outs[2 * i + b][...] = nt_dot(lefts[b], right).reshape(half, tall, wide).astype(bf16)


def product_kernel(offsets, left_ref, right_ref, *outs):
    give_blocks(left_ref, right_ref, outs, offsets)


def back_kernel(offsets, evens, pre_ref, back_ref, left_ref, *refs):
    count = len(offsets)
    weights, outs, out_ref = refs[:count], refs[count:-1], refs[-1]
    me = lax.axis_index("feat")
    wide = weights[0].shape[1]
    place = [pl.ds(pl.multiple_of((me ^ o) * wide, wide), wide) for o in offsets]
    for at in place:
        total = None
        for w_ref, rows in zip(weights, place):
            term = lax.dot_general(
                w_ref[1, :, at], back_ref[rows, :], (((0,), (0,)), ((), ())), preferred_element_type=f32
            )
            total = term if total is None else total + term
        pre = pre_ref[at, :]
        sigma = jax.nn.sigmoid(pre)
        out_ref[at, :] = (total * sigma * (1.0 + pre * (1.0 - sigma))).astype(bf16)
    give_blocks(left_ref, out_ref, outs, evens)


def quarter_kernel(offsets, left_ref, right_ref, *refs):
    spots = 2 * len(offsets)
    came, outs = refs[:spots], refs[spots:]
    me = lax.axis_index("feat")
    half, tall, wide = outs[0].shape
    lefts = side_rows(left_ref, tall)
    for i, o in enumerate(offsets):
        right = right_ref[pl.ds(pl.multiple_of((me ^ o) * wide, wide), wide), :]
        for b in range(2):
            total = nt_dot(lefts[b], right).reshape(half, tall, wide) + came[2 * i + b][...].astype(f32)
            outs[2 * i + b][...] = total.astype(outs[2 * i + b].dtype)


def split_kernel(keep_ref, *refs):
    half = keep_ref.shape[0]
    came, mine_ref, outs = refs[:-half], refs[-half], refs[len(refs) - half + 1 :]
    me = lax.axis_index("nodes") // 2
    for i, o_ref in enumerate((mine_ref,) + outs):
        total = keep_ref[me ^ i]
        for ref in came:
            total = total + ref[me ^ i].astype(f32)
        o_ref[...] = total.astype(o_ref.dtype)


def even_offsets():
    return list(range(0, lax.axis_size("feat"), 2))


def give_shapes(hidden_width):
    nodes, count = lax.axis_size("nodes"), lax.axis_size("feat")
    return [((nodes // 2, hidden_width // nodes, hidden_width // count), bf16)] * count


def quarters(left, right, *given):
    swapped = [swap(v, "feat", 1) for v in given]
    shape = given[0].shape
    return call(
        functools.partial(quarter_kernel, even_offsets()),
        [(shape, f32)] + [(shape, bf16)] * (len(given) - 1),
        [vmem] * (2 + len(given)),
        (left, right, *swapped),
        sent=tuple(range(1, len(given))),
    )


def pass_quarters(mine, *rest, late=None):
    nodes, feat_count = lax.axis_size("nodes"), lax.axis_size("feat")
    spots = [(o, b) for o in even_offsets() for b in range(2)][1:]
    ring = range(nodes * feat_count)
    if late is not None:
        rest = [after(v, late) if o == 0 else v for v, (o, b) in zip(rest, spots)]
    moved = [
        lax.ppermute(v, ("nodes", "feat"), [(i, i ^ (b * feat_count + o)) for i in ring]) for v, (o, b) in zip(rest, spots)
    ]
    return mine, *moved


def grad_sum(flops, keep, *came):
    half, tall, wide = keep.shape
    mine, *rest = call(
        split_kernel,
        [((tall, wide), f32)] + [((tall, wide), bf16)] * (half - 1),
        [vmem] + [far] * len(came),
        (keep, *came),
        flops=flops,
        sent=tuple(range(1, half)),
    )
    for i, part in enumerate(rest):
        mine = mine + swap(part, "nodes", 2 * (i + 1)).astype(f32)
    return mine


def on_device(
    features, ghosts, slots, tile_ids, degrees, tile_table, weight_one, weight_two, cotangent
):
    nodes, feat_count = lax.axis_size("nodes"), lax.axis_size("feat")
    every = ("feat", "nodes")
    per, width_k = slots.shape
    size = tile_table.shape[1]
    rows, wide = features.shape
    held = rows // feat_count
    hidden_width = wide * feat_count
    exchange = lambda v, axes: lax.all_to_all(v, axes, split_axis=0, concat_axis=0, tiled=True)

    sent = pack(features, ghosts, slots, tile_ids, degrees, nodes, size)
    came = exchange(sent, "nodes")
    packed = pack_parts(after(cotangent, sent), nodes, size)
    first, second = after((weight_one, weight_two), sent)
    weights, offsets = gather_parts(jnp.stack([first.T, second.T]), "feat")

    spread, ids = spread_first(after(came, packed), tile_table, per, width_k, feat_count)
    cot_parts = [packed[0]] + [swap(p, "nodes", i) for i, p in enumerate(packed) if i]
    agg = exchange(after(spread, *cot_parts), every).reshape(hidden_width, held)
    back = spread_back(cot_parts, ids, tile_table, per, width_k, feat_count)
    agg = after(agg, back)
    back = exchange(back, every).reshape(hidden_width, held)

    parts = len(offsets)
    pre, hidden, wide_out = call(
        functools.partial(project_kernel, offsets),
        [((hidden_width, held), f32)] + [((hidden_width, held), bf16)] * 2,
        [far] + [vmem] * parts,
        (agg, *weights),
        flops=4 * hidden_width * hidden_width * held,
        moved=4 << 20,
        sent=(2,),
    )
    wide_out = after(wide_out, back)
    out_t = exchange(wide_out.reshape(feat_count * nodes, wide // nodes, held), every)

    evens = even_offsets()
    give_two = call(
        functools.partial(product_kernel, evens),
        give_shapes(hidden_width),
        [vmem] * 2,
        (hidden, back),
        sent=tuple(range(parts)),
    )
    *give_one, back_pre = call(
        functools.partial(back_kernel, offsets, evens),
        give_shapes(hidden_width) + [((hidden_width, held), bf16)],
        [vmem] * (3 + parts),
        (pre, back, agg, *weights),
        sent=tuple(range(parts)),
    )
    halves_two = quarters(hidden, back, *give_two)
    halves_one = quarters(agg, back_pre, *give_one)
    quarters_two = pass_quarters(*halves_two)
    last = spread_last(out_t, ids, tile_table, per, width_k, nodes)
    out_n = exchange(last, "nodes")
    quarters_one = pass_quarters(*halves_one, late=None)
    grad_two = grad_sum(0, *after(quarters_two, last))
    grad_one = grad_sum(20 << 30, *after(quarters_one, last))
    output = out_n.reshape(wide, rows).T
    return (output, grad_one, grad_two)


def solution(mesh):
    return jax.shard_map(
        on_device,
        mesh=mesh,
        in_specs=(
            P("nodes", "feat"),
            P("nodes", None),
            P("nodes", None),
            P("nodes", None),
            P("nodes"),
            P(),
            P(None, "feat"),
            P(None, "feat"),
            P("nodes", "feat"),
        ),
        out_specs=(P("nodes", "feat"), P("nodes", "feat"), P("nodes", "feat")),
        check_vma=False,
    )
```

```python
import functools

import jax
import jax.numpy as jnp
from jax import lax
from jax.experimental import pallas as pl
from jax.experimental.pallas import tpu as pltpu
from jax.sharding import PartitionSpec as P

unroll = 4
tile_step = 4
meta_rows = 16
bf16, f32 = jnp.bfloat16, jnp.float32
vmem = pl.BlockSpec(memory_space=pltpu.VMEM)
smem = pl.BlockSpec(memory_space=pltpu.SMEM)
far = object()


def nt_dot(a, b):
    return lax.dot_general(a, b, (((1,), (1,)), ((), ())), preferred_element_type=f32)


def call(body, outs, in_specs, args, scratch=(), flops=0, limit=16, moved=0, sent=()):
    return pl.pallas_call(
        body,
        out_shape=[(pltpu.HBM if i in sent else jax.ShapeDtypeStruct)(s, d) for i, (s, d) in enumerate(outs)],
        in_specs=[vmem if spec is far else spec for spec in in_specs],
        out_specs=[vmem] * len(outs),
        scratch_shapes=list(scratch),
        compiler_params=pltpu.CompilerParams(vmem_limit_bytes=limit * 1024 * 1024),
        cost_estimate=pl.CostEstimate(flops=flops, bytes_accessed=moved, transcendentals=0),
    )(*[pltpu.with_memory_space_constraint(v, pltpu.HBM) if spec is far else v for v, spec in zip(args, in_specs)])


def after(values, *earlier):
    return lax.optimization_barrier((values, earlier))[0]


def meta_tile(ghost_at, degree_at, slots, tile_ids, owners, held, size):
    per, width_k = slots.shape
    near = jnp.zeros((per, width_k), jnp.int32)
    for s in range(owners * held):
        near = jnp.where(slots == s, (s // held) * per + ghost_at(s // held, s % held), near)
    row = lax.broadcasted_iota(jnp.int32, (per, size), 0)
    lane = lax.broadcasted_iota(jnp.int32, (per, size), 1)
    degree = jnp.zeros((per, size), jnp.int32)
    for r in range(per):
        degree = jnp.where(row == r, degree_at(r), degree)
    widen = lambda v: jnp.concatenate([v, jnp.zeros((per, size - width_k), jnp.int32)], axis=1)
    top = jnp.where(lane == width_k, degree, widen(near))
    return jnp.concatenate([top, widen(tile_ids)], axis=0).astype(f32).astype(bf16)


def pack_kernel(owners, held, ghosts, degrees, slots_ref, tiles_ref, feat_ref, o_ref):
    nodes, rows, size = o_ref.shape
    width = feat_ref.shape[1] // nodes
    per = feat_ref.shape[0] // size
    for b in range(per):
        turned = feat_ref[b * size : (b + 1) * size, :].T
        for n in range(nodes):
            o_ref[n, b * width : (b + 1) * width, :] = turned[n * width : (n + 1) * width]
    tile = meta_tile(
        lambda p, c: ghosts[c : c + 1, p : p + 1], lambda r: degrees[r], slots_ref[...], tiles_ref[...], owners, held, size
    )
    for n in range(nodes):
        o_ref[n, rows - meta_rows :, :] = tile


def turn_blocks(values, nodes, size):
    per, width = values.shape[0] // size, values.shape[1] // nodes
    return values.reshape(per, size, nodes, width).transpose(2, 0, 3, 1).reshape(nodes, per * width, size)


def pack(features, ghosts, slots, tile_ids, degrees, nodes, size):
    owners, held = ghosts.shape
    per = slots.shape[0]
    width = features.shape[1] // nodes
    if width % 16:
        tile = meta_tile(lambda p, c: ghosts[p, c], lambda r: degrees[r], slots, tile_ids, owners, held, size)
        tile = jnp.broadcast_to(tile, (nodes,) + tile.shape)
        return jnp.concatenate([turn_blocks(features, nodes, size), tile], axis=1)
    return call(
        functools.partial(pack_kernel, owners, held),
        [((nodes, per * width + meta_rows, size), bf16)],
        [far, smem, far, far, far],
        (ghosts.T, degrees, slots, tile_ids, features),
        sent=(0,),
    )[0]


def turn_kernel(v_ref, *refs):
    outs, turned_ref = refs[:-1], refs[-1]
    size = outs[0].shape[1]
    per = v_ref.shape[0] // size
    width = v_ref.shape[1] // len(outs)
    me = lax.axis_index("nodes")
    for b in range(per):
        turned_ref[b] = v_ref[b * size : (b + 1) * size, :].T
    for i, o_ref in enumerate(outs):
        at = pl.ds(pl.multiple_of((me ^ i) * width, width), width)
        for b in range(per):
            o_ref[b * width : (b + 1) * width, :] = turned_ref[b, at, :]


def pack_parts(values, nodes, size):
    per, width = values.shape[0] // size, values.shape[1] // nodes
    if width % 16:
        me = lax.axis_index("nodes")
        turned = turn_blocks(values, nodes, size)
        return [lax.dynamic_index_in_dim(turned, me ^ i, 0, keepdims=False) for i in range(nodes)]
    return call(
        turn_kernel,
        [((per * width, size), bf16)] * nodes,
        [vmem],
        (values,),
        [pltpu.VMEM((per, values.shape[1], size), bf16)],
        sent=tuple(range(nodes)),
    )


def form_products(lefts, count, width, tiles_ref, p_ref, transposed):
    tile_count, size = tiles_ref.shape[0], tiles_ref.shape[1]

    def step(turn, carry):
        some = tiles_ref[pl.ds(tile_step * turn, tile_step)]
        if transposed:
            right = jnp.concatenate([some[i] for i in range(tile_step)], axis=1)
        else:
            right = some.reshape(tile_step * size, size)
        for first, load in lefts:
            left = load()
            res = jnp.dot(left, right, preferred_element_type=f32) if transposed else nt_dot(left, right)
            group = left.shape[0] // width
            for i in range(tile_step):
                part = res[:, i * size : (i + 1) * size].reshape(group, width, size)
                p_ref[pl.ds((tile_step * turn + i) * count + first, group)] = part
        return carry

    lax.fori_loop(0, tile_count // tile_step, step, 0)
    p_ref[tile_count * count] = jnp.zeros((width, size), f32)


def sum_entries(pick, r, width_k, p_ref):
    terms = [p_ref[pick[r, k]] for k in range(width_k)]
    while len(terms) > 1:
        terms = [terms[i] + terms[i + 1] for i in range(0, len(terms) - 1, 2)] + terms[len(terms) & ~1 :]
    return terms[0]


def first_kernel(per, width_k, v_ref, tiles_ref, o_ref, ids_ref, weight_ref, pick, p_ref, sem):
    nodes, _, size = v_ref.shape
    width = o_ref.shape[1]
    share = o_ref.shape[2] // size
    count = nodes * per
    span = per * width
    empty = tiles_ref.shape[0] * count
    lane = lax.broadcasted_iota(jnp.int32, (per, size), 1)
    row = lax.broadcasted_iota(jnp.int32, (per, size), 0)
    for n in range(nodes):
        raw = v_ref[n, span:, :].astype(f32).astype(jnp.int32)
        links, tile = raw[:per], raw[per:]
        degree = jnp.broadcast_to(links[:, width_k : width_k + 1], (per, size))
        live = lane < degree
        block = slice(n * per, (n + 1) * per)
        ids_ref[0, block] = jnp.where(live, tile * count + links, empty)
        ids_ref[1, block] = jnp.where(live, tile * count + (row + n * per), empty)
        ids_ref[2, block] = links
        weight_ref[block] = lax.rsqrt(degree.astype(f32))
    copy = pltpu.make_async_copy(ids_ref.at[0], pick, sem)
    copy.start()
    lefts = [(n * per, lambda n=n: v_ref[n, :span, :]) for n in range(nodes)]
    form_products(lefts, count, width, tiles_ref, p_ref, False)
    copy.wait()

    def rows(n, carry):
        for b in range(per):
            r = n * per + b
            own = v_ref[n, b * width : (b + 1) * width, :].astype(f32)
            j = b % share
            value = (own + weight_ref[pl.ds(r, 1), :] * sum_entries(pick, r, width_k, p_ref)).astype(bf16)
            o_ref[(b // share) * nodes + n, :, j * size : (j + 1) * size] = value
        return carry

    lax.fori_loop(0, nodes, rows, 0)


def back_spread_kernel(per, width_k, nodes, pick, near, weight_ref, tiles_ref, *refs):
    parts, o_ref, p_ref, sums = refs[:nodes], refs[nodes], refs[nodes + 1], refs[nodes + 2 :]
    me = lax.axis_index("nodes")
    size = tiles_ref.shape[1]
    width = o_ref.shape[1]
    share = o_ref.shape[2] // size
    count = nodes * per
    block = [pl.multiple_of((me ^ i) * per, per) for i in range(nodes)]
    form_products(
        [(block[i], lambda i=i: parts[i][...]) for i in range(nodes)], count, width, tiles_ref, p_ref, True
    )
    for i in range(nodes):
        sums[0][pl.ds(block[i], per)] = parts[i][...].astype(f32).reshape(per, width, size)
    for total in sums[1:]:
        total[...] = jnp.zeros(total.shape, f32)

    def entry_row(r, carry):
        scale = weight_ref[pl.ds(r, 1), :]

        def chunk(c, inner):
            base = c * unroll
            for u in range(unroll):
                g = near[r, base + u]
                sums[u][g] = sums[u][g] + scale * p_ref[pick[r, base + u]]
            return inner

        return lax.fori_loop(0, (near[r, width_k] + (unroll - 1)) // unroll, chunk, carry)

    lax.fori_loop(0, count, entry_row, 0)

    def rows(n, carry):
        for b in range(per):
            r = n * per + b
            j = b % share
            value = ((sums[0][r] + sums[1][r]) + (sums[2][r] + sums[3][r])).astype(bf16)
            o_ref[(b // share) * nodes + n, :, j * size : (j + 1) * size] = value
        return carry

    lax.fori_loop(0, nodes, rows, 0)


def last_kernel(per, width_k, pick, weight_ref, v_ref, tiles_ref, o_ref, x_ref, p_ref):
    nodes = o_ref.shape[0]
    count, width, size = x_ref.shape
    share = v_ref.shape[2] // size
    for f in range(per // share):
        for n in range(nodes):
            for j in range(share):
                x_ref[n * per + f * share + j] = v_ref[f * nodes + n, :, j * size : (j + 1) * size]
    group = 256 // width
    lefts = [
        (first, lambda first=first: x_ref[first : first + group].reshape(group * width, size))
        for first in range(0, count, group)
    ]
    form_products(lefts, count, width, tiles_ref, p_ref, False)

    def rows(n, carry):
        for b in range(per):
            r = n * per + b
            acc = sum_entries(pick, r, width_k, p_ref)
            value = x_ref[r].astype(f32) + weight_ref[pl.ds(r, 1), :] * acc
            o_ref[n, :, b * size : (b + 1) * size] = value.astype(bf16)
        return carry

    lax.fori_loop(0, nodes, rows, 0)


def plain_spread(x, ids, tiles, transposed):
    near, tile_ids, degrees = ids
    rows = jnp.arange(x.shape[0])
    kind = "gfi,tij->tgfj" if transposed else "gfj,tij->tgfi"
    products = jnp.einsum(kind, x, tiles, preferred_element_type=f32)
    weight = lax.rsqrt(degrees.astype(f32))

    def step(k, acc):
        g, t = near[:, k], tile_ids[:, k]
        scale = jnp.where(k < degrees, weight, 0.0)[:, None, None]
        if transposed:
            return acc.at[g].add(scale * products[t, rows])
        return acc + scale * products[t, g]

    return lax.fori_loop(0, near.shape[1], step, x.astype(f32)).astype(bf16)


def product_flops(tiles, count, width):
    return 2 * tiles.shape[0] * count * width * tiles.shape[1] * tiles.shape[1]


def product_scratch(tiles, count, width):
    return pltpu.VMEM((tiles.shape[0] * count + 1, width, tiles.shape[1]), f32)


def spread_first(v, tiles, per, width_k, feat_count):
    nodes, rows, size = v.shape
    width = (rows - meta_rows) // per
    count, share = nodes * per, per // feat_count
    if width % 16:
        raw = v[:, rows - meta_rows :, :].astype(jnp.int32)
        links = raw[:, :per].reshape(count, size)
        ids = (links[:, :width_k], raw[:, per:].reshape(count, size)[:, :width_k], links[:, width_k])
        out = plain_spread(v[:, : rows - meta_rows].reshape(count, width, size), ids, tiles, False)
        out = out.reshape(nodes, feat_count, share, width, size).transpose(1, 0, 3, 2, 4)
        return out.reshape(feat_count * nodes, width, share * size), ids
    return_ids = ((3, count, size), jnp.int32)
    out, ids, weight = call(
        functools.partial(first_kernel, per, width_k),
        [((feat_count * nodes, width, share * size), bf16), return_ids, ((count, size), f32)],
        [vmem, vmem],
        (v, tiles),
        [
            pltpu.SMEM((count, size), jnp.int32),
            product_scratch(tiles, count, width),
            pltpu.SemaphoreType.DMA,
        ],
        0,
        28,
        sent=(0, 1, 2),
    )
    return out, (ids[0], ids[1], ids[2], weight)


def spread_back(parts, ids, tiles, per, width_k, feat_count):
    nodes, size = len(parts), tiles.shape[1]
    width, count, share = parts[0].shape[0] // per, len(parts) * per, per // feat_count
    if width % 16:
        order = lax.axis_index("nodes") ^ jnp.arange(nodes)
        out = plain_spread(jnp.stack(parts)[order].reshape(count, width, size), ids, tiles, True)
        out = out.reshape(nodes, feat_count, share, width, size).transpose(1, 0, 3, 2, 4)
        return out.reshape(feat_count * nodes, width, share * size)
    _, pick_back, near, weight = ids
    return call(
        functools.partial(back_spread_kernel, per, width_k, nodes),
        [((feat_count * nodes, width, share * size), bf16)],
        [smem, smem, vmem, vmem, vmem] + [far] * (nodes - 1),
        (pick_back, near, weight, tiles, *parts),
        [product_scratch(tiles, count, width)] + [pltpu.VMEM((count, width, size), f32)] * unroll,
        product_flops(tiles, count, width),
        28,
        4 << 20,
        (0,),
    )[0]


def spread_last(v, ids, tiles, per, width_k, nodes):
    size = tiles.shape[1]
    every, width, held = v.shape
    feat_count, share, count = every // nodes, held // size, nodes * per
    if width % 16:
        x = v.reshape(feat_count, nodes, width, share, size).transpose(1, 0, 3, 2, 4).reshape(count, width, size)
        out = plain_spread(x, ids, tiles, False)
        return out.reshape(nodes, per, width, size).transpose(0, 2, 1, 3).reshape(nodes, width, per * size)
    pick, _, _, weight = ids
    return call(
        functools.partial(last_kernel, per, width_k),
        [((nodes, width, per * size), bf16)],
        [smem, vmem, vmem, vmem],
        (pick, weight, v, tiles),
        [pltpu.VMEM((count, width, size), bf16), product_scratch(tiles, count, width)],
        10 * product_flops(tiles, count, width),
        28,
        sent=(0,),
    )[0]


def swap(values, axis, mask):
    return lax.ppermute(values, axis, [(i, i ^ mask) for i in range(lax.axis_size(axis))])


def gather_parts(values, axis):
    parts, offsets = [values], [0]
    bit = lax.axis_size(axis) // 2
    while bit:
        parts = parts + [swap(v, axis, bit) for v in parts]
        offsets = offsets + [o ^ bit for o in offsets]
        bit //= 2
    return parts, offsets


def project_kernel(offsets, agg_ref, *refs):
    count = len(offsets)
    weights, (pre_ref, hidden_ref, y_ref) = refs[:count], refs[count:]
    me = lax.axis_index("feat")
    wide = weights[0].shape[1]
    agg = agg_ref[...]
    place = [pl.ds(pl.multiple_of((me ^ o) * wide, wide), wide) for o in offsets]
    for at, w_ref in zip(place, weights):
        pre = jnp.dot(w_ref[0], agg, preferred_element_type=f32)
        pre_ref[at, :] = pre
        hidden_ref[at, :] = (pre * jax.nn.sigmoid(pre)).astype(bf16)
    hidden = hidden_ref[...]
    for at, w_ref in zip(place, weights):
        y_ref[at, :] = jnp.dot(w_ref[1], hidden, preferred_element_type=f32).astype(bf16)


def side_rows(left_ref, tall):
    side = lax.axis_index("nodes") % 2
    pick = lambda row: left_ref[pl.ds(pl.multiple_of(row * tall, tall), tall), :]
    half = left_ref.shape[0] // (2 * tall)
    return [jnp.concatenate([pick(2 * h + (side ^ b)) for h in range(half)], axis=0) for b in range(2)]


def give_blocks(left_ref, right_ref, outs, offsets):
    me = lax.axis_index("feat")
    half, tall, wide = outs[0].shape
    lefts = side_rows(left_ref, tall)
    for i, o in enumerate(offsets):
        right = right_ref[pl.ds(pl.multiple_of((me ^ o ^ 1) * wide, wide), wide), :]
        for b in range(2):
            outs[2 * i + b][...] = nt_dot(lefts[b], right).reshape(half, tall, wide).astype(bf16)


def product_kernel(offsets, left_ref, right_ref, *outs):
    give_blocks(left_ref, right_ref, outs, offsets)


def back_kernel(offsets, evens, pre_ref, back_ref, left_ref, *refs):
    count = len(offsets)
    weights, outs, out_ref = refs[:count], refs[count:-1], refs[-1]
    me = lax.axis_index("feat")
    wide = weights[0].shape[1]
    place = [pl.ds(pl.multiple_of((me ^ o) * wide, wide), wide) for o in offsets]
    for at in place:
        total = None
        for w_ref, rows in zip(weights, place):
            term = lax.dot_general(
                w_ref[1, :, at], back_ref[rows, :], (((0,), (0,)), ((), ())), preferred_element_type=f32
            )
            total = term if total is None else total + term
        pre = pre_ref[at, :]
        sigma = jax.nn.sigmoid(pre)
        out_ref[at, :] = (total * sigma * (1.0 + pre * (1.0 - sigma))).astype(bf16)
    give_blocks(left_ref, out_ref, outs, evens)


def quarter_kernel(offsets, left_ref, right_ref, *refs):
    spots = 2 * len(offsets)
    came, outs = refs[:spots], refs[spots:]
    me = lax.axis_index("feat")
    half, tall, wide = outs[0].shape
    lefts = side_rows(left_ref, tall)
    for i, o in enumerate(offsets):
        right = right_ref[pl.ds(pl.multiple_of((me ^ o) * wide, wide), wide), :]
        for b in range(2):
            total = nt_dot(lefts[b], right).reshape(half, tall, wide) + came[2 * i + b][...].astype(f32)
            outs[2 * i + b][...] = total.astype(outs[2 * i + b].dtype)


def split_kernel(keep_ref, *refs):
    half = keep_ref.shape[0]
    came, mine_ref, outs = refs[:-half], refs[-half], refs[len(refs) - half + 1 :]
    me = lax.axis_index("nodes") // 2
    for i, o_ref in enumerate((mine_ref,) + outs):
        total = keep_ref[me ^ i]
        for ref in came:
            total = total + ref[me ^ i].astype(f32)
        o_ref[...] = total.astype(o_ref.dtype)


def even_offsets():
    return list(range(0, lax.axis_size("feat"), 2))


def give_shapes(hidden_width):
    nodes, count = lax.axis_size("nodes"), lax.axis_size("feat")
    return [((nodes // 2, hidden_width // nodes, hidden_width // count), bf16)] * count


def quarters(left, right, *given):
    swapped = [swap(v, "feat", 1) for v in given]
    shape = given[0].shape
    return call(
        functools.partial(quarter_kernel, even_offsets()),
        [(shape, f32)] + [(shape, bf16)] * (len(given) - 1),
        [vmem] * (2 + len(given)),
        (left, right, *swapped),
        sent=tuple(range(1, len(given))),
    )


def pass_quarters(mine, *rest, late=None):
    nodes, feat_count = lax.axis_size("nodes"), lax.axis_size("feat")
    spots = [(o, b) for o in even_offsets() for b in range(2)][1:]
    ring = range(nodes * feat_count)
    if late is not None:
        rest = [after(v, late) if o == 0 else v for v, (o, b) in zip(rest, spots)]
    moved = [
        lax.ppermute(v, ("nodes", "feat"), [(i, i ^ (b * feat_count + o)) for i in ring]) for v, (o, b) in zip(rest, spots)
    ]
    return mine, *moved


def grad_sum(flops, keep, *came):
    half, tall, wide = keep.shape
    mine, *rest = call(
        split_kernel,
        [((tall, wide), f32)] + [((tall, wide), bf16)] * (half - 1),
        [vmem] * (1 + len(came)),
        (keep, *came),
        flops=flops,
        sent=tuple(range(1, half)),
    )
    for i, part in enumerate(rest):
        mine = mine + swap(part, "nodes", 2 * (i + 1)).astype(f32)
    return mine


def on_device(
    features, ghosts, slots, tile_ids, degrees, tile_table, weight_one, weight_two, cotangent
):
    nodes, feat_count = lax.axis_size("nodes"), lax.axis_size("feat")
    every = ("feat", "nodes")
    per, width_k = slots.shape
    size = tile_table.shape[1]
    rows, wide = features.shape
    held = rows // feat_count
    hidden_width = wide * feat_count
    exchange = lambda v, axes: lax.all_to_all(v, axes, split_axis=0, concat_axis=0, tiled=True)

    sent = pack(features, ghosts, slots, tile_ids, degrees, nodes, size)
    came = exchange(sent, "nodes")
    packed = pack_parts(after(cotangent, sent), nodes, size)
    first, second = after((weight_one, weight_two), sent)
    weights, offsets = gather_parts(jnp.stack([first.T, second.T]), "feat")

    spread, ids = spread_first(after(came, packed), tile_table, per, width_k, feat_count)
    cot_parts = [packed[0]] + [swap(p, "nodes", i) for i, p in enumerate(packed) if i]
    agg = exchange(after(spread, *cot_parts), every).reshape(hidden_width, held)
    back = spread_back(cot_parts, ids, tile_table, per, width_k, feat_count)
    agg = after(agg, back)
    back = exchange(back, every).reshape(hidden_width, held)

    parts = len(offsets)
    pre, hidden, wide_out = call(
        functools.partial(project_kernel, offsets),
        [((hidden_width, held), f32)] + [((hidden_width, held), bf16)] * 2,
        [vmem] * (1 + parts),
        (agg, *weights),
        flops=4 * hidden_width * hidden_width * held,
        moved=4 << 20,
        sent=(0, 2),
    )
    wide_out = after(wide_out, back)
    out_t = exchange(wide_out.reshape(feat_count * nodes, wide // nodes, held), every)

    evens = even_offsets()
    give_two = call(
        functools.partial(product_kernel, evens),
        give_shapes(hidden_width),
        [vmem] * 2,
        (hidden, back),
        sent=tuple(range(parts)),
    )
    *give_one, back_pre = call(
        functools.partial(back_kernel, offsets, evens),
        give_shapes(hidden_width) + [((hidden_width, held), bf16)],
        [far] + [vmem] * (2 + parts),
        (pre, back, agg, *weights),
        sent=tuple(range(parts)),
    )
    halves_two = quarters(hidden, back, *give_two)
    halves_one = quarters(agg, back_pre, *give_one)
    quarters_two = pass_quarters(*halves_two)
    last = spread_last(out_t, ids, tile_table, per, width_k, nodes)
    out_n = exchange(last, "nodes")
    quarters_one = pass_quarters(*halves_one, late=None)
    grad_two = grad_sum(0, *after(quarters_two, last))
    grad_one = grad_sum(20 << 30, *after(quarters_one, last))
    output = out_n.reshape(wide, rows).T
    return (output, grad_one, grad_two)


def solution(mesh):
    return jax.shard_map(
        on_device,
        mesh=mesh,
        in_specs=(
            P("nodes", "feat"),
            P("nodes", None),
            P("nodes", None),
            P("nodes", None),
            P("nodes"),
            P(),
            P(None, "feat"),
            P(None, "feat"),
            P("nodes", "feat"),
        ),
        out_specs=(P("nodes", "feat"), P("nodes", "feat"), P("nodes", "feat")),
        check_vma=False,
    )
```

```python
import functools

import jax
import jax.numpy as jnp
from jax import lax
from jax.experimental import pallas as pl
from jax.experimental.pallas import tpu as pltpu
from jax.sharding import PartitionSpec as P

unroll = 4
tile_step = 8
meta_rows = 16
bf16, f32 = jnp.bfloat16, jnp.float32
vmem = pl.BlockSpec(memory_space=pltpu.VMEM)
smem = pl.BlockSpec(memory_space=pltpu.SMEM)
far = object()


def nt_dot(a, b):
    return lax.dot_general(a, b, (((1,), (1,)), ((), ())), preferred_element_type=f32)


def call(body, outs, in_specs, args, scratch=(), flops=0, limit=16, moved=0, sent=()):
    return pl.pallas_call(
        body,
        out_shape=[(pltpu.HBM if i in sent else jax.ShapeDtypeStruct)(s, d) for i, (s, d) in enumerate(outs)],
        in_specs=[vmem if spec is far else spec for spec in in_specs],
        out_specs=[vmem] * len(outs),
        scratch_shapes=list(scratch),
        compiler_params=pltpu.CompilerParams(vmem_limit_bytes=limit * 1024 * 1024),
        cost_estimate=pl.CostEstimate(flops=flops, bytes_accessed=moved, transcendentals=0),
    )(*[pltpu.with_memory_space_constraint(v, pltpu.HBM) if spec is far else v for v, spec in zip(args, in_specs)])


def after(values, *earlier):
    return lax.optimization_barrier((values, earlier))[0]


def meta_tile(ghost_at, degree_at, slots, tile_ids, owners, held, size):
    per, width_k = slots.shape
    near = jnp.zeros((per, width_k), jnp.int32)
    for s in range(owners * held):
        near = jnp.where(slots == s, (s // held) * per + ghost_at(s // held, s % held), near)
    row = lax.broadcasted_iota(jnp.int32, (per, size), 0)
    lane = lax.broadcasted_iota(jnp.int32, (per, size), 1)
    degree = jnp.zeros((per, size), jnp.int32)
    for r in range(per):
        degree = jnp.where(row == r, degree_at(r), degree)
    widen = lambda v: jnp.concatenate([v, jnp.zeros((per, size - width_k), jnp.int32)], axis=1)
    top = jnp.where(lane == width_k, degree, widen(near))
    return jnp.concatenate([top, widen(tile_ids)], axis=0).astype(f32).astype(bf16)


def pack_kernel(owners, held, ghosts, degrees, slots_ref, tiles_ref, feat_ref, o_ref):
    nodes, rows, size = o_ref.shape
    width = feat_ref.shape[1] // nodes
    per = feat_ref.shape[0] // size
    for b in range(per):
        turned = feat_ref[b * size : (b + 1) * size, :].T
        for n in range(nodes):
            o_ref[n, b * width : (b + 1) * width, :] = turned[n * width : (n + 1) * width]
    tile = meta_tile(
        lambda p, c: ghosts[c : c + 1, p : p + 1], lambda r: degrees[r], slots_ref[...], tiles_ref[...], owners, held, size
    )
    for n in range(nodes):
        o_ref[n, rows - meta_rows :, :] = tile


def turn_blocks(values, nodes, size):
    per, width = values.shape[0] // size, values.shape[1] // nodes
    return values.reshape(per, size, nodes, width).transpose(2, 0, 3, 1).reshape(nodes, per * width, size)


def pack(features, ghosts, slots, tile_ids, degrees, nodes, size):
    owners, held = ghosts.shape
    per = slots.shape[0]
    width = features.shape[1] // nodes
    if width % 16:
        tile = meta_tile(lambda p, c: ghosts[p, c], lambda r: degrees[r], slots, tile_ids, owners, held, size)
        tile = jnp.broadcast_to(tile, (nodes,) + tile.shape)
        return jnp.concatenate([turn_blocks(features, nodes, size), tile], axis=1)
    return call(
        functools.partial(pack_kernel, owners, held),
        [((nodes, per * width + meta_rows, size), bf16)],
        [far, smem, far, far, far],
        (ghosts.T, pltpu.with_memory_space_constraint(degrees, pltpu.HBM), slots, tile_ids, features),
        sent=(0,),
    )[0]


def turn_kernel(v_ref, *refs):
    outs, turned_ref = refs[:-1], refs[-1]
    size = outs[0].shape[1]
    per = v_ref.shape[0] // size
    width = v_ref.shape[1] // len(outs)
    me = lax.axis_index("nodes")
    for b in range(per):
        turned_ref[b] = v_ref[b * size : (b + 1) * size, :].T
    for i, o_ref in enumerate(outs):
        at = pl.ds(pl.multiple_of((me ^ i) * width, width), width)
        for b in range(per):
            o_ref[b * width : (b + 1) * width, :] = turned_ref[b, at, :]


def pack_parts(values, nodes, size):
    per, width = values.shape[0] // size, values.shape[1] // nodes
    if width % 16:
        me = lax.axis_index("nodes")
        turned = turn_blocks(values, nodes, size)
        return [lax.dynamic_index_in_dim(turned, me ^ i, 0, keepdims=False) for i in range(nodes)]
    return call(
        turn_kernel,
        [((per * width, size), bf16)] * nodes,
        [vmem],
        (values,),
        [pltpu.VMEM((per, values.shape[1], size), bf16)],
        sent=tuple(range(nodes)),
    )


def form_products(lefts, count, width, tiles_ref, p_ref, transposed):
    tile_count, size = tiles_ref.shape[0], tiles_ref.shape[1]

    def step(turn, carry):
        some = tiles_ref[pl.ds(tile_step * turn, tile_step)]
        if transposed:
            right = jnp.concatenate([some[i] for i in range(tile_step)], axis=1)
        else:
            right = some.reshape(tile_step * size, size)
        for first, load in lefts:
            left = load()
            res = jnp.dot(left, right, preferred_element_type=f32) if transposed else nt_dot(left, right)
            group = left.shape[0] // width
            for i in range(tile_step):
                part = res[:, i * size : (i + 1) * size].reshape(group, width, size)
                p_ref[pl.ds((tile_step * turn + i) * count + first, group)] = part
        return carry

    lax.fori_loop(0, tile_count // tile_step, step, 0)
    p_ref[tile_count * count] = jnp.zeros((width, size), f32)


def sum_entries(pick, r, width_k, p_ref):
    terms = [p_ref[pick[r, k]] for k in range(width_k)]
    while len(terms) > 1:
        terms = [terms[i] + terms[i + 1] for i in range(0, len(terms) - 1, 2)] + terms[len(terms) & ~1 :]
    return terms[0]


def first_kernel(per, width_k, v_ref, tiles_ref, o_ref, ids_ref, weight_ref, pick, p_ref, sem):
    nodes, _, size = v_ref.shape
    width = o_ref.shape[1]
    share = o_ref.shape[2] // size
    count = nodes * per
    span = per * width
    empty = tiles_ref.shape[0] * count
    lane = lax.broadcasted_iota(jnp.int32, (per, size), 1)
    row = lax.broadcasted_iota(jnp.int32, (per, size), 0)
    for n in range(nodes):
        raw = v_ref[n, span:, :].astype(f32).astype(jnp.int32)
        links, tile = raw[:per], raw[per:]
        degree = jnp.broadcast_to(links[:, width_k : width_k + 1], (per, size))
        live = lane < degree
        block = slice(n * per, (n + 1) * per)
        ids_ref[0, block] = jnp.where(live, tile * count + links, empty)
        ids_ref[1, block] = jnp.where(live, tile * count + (row + n * per), empty)
        ids_ref[2, block] = links
        weight_ref[block] = lax.rsqrt(degree.astype(f32))
    copy = pltpu.make_async_copy(ids_ref.at[0], pick, sem)
    copy.start()
    lefts = [(n * per, lambda n=n: v_ref[n, :span, :]) for n in range(nodes)]
    form_products(lefts, count, width, tiles_ref, p_ref, False)
    copy.wait()

    def rows(n, carry):
        for b in range(per):
            r = n * per + b
            own = v_ref[n, b * width : (b + 1) * width, :].astype(f32)
            j = b % share
            value = (own + weight_ref[pl.ds(r, 1), :] * sum_entries(pick, r, width_k, p_ref)).astype(bf16)
            o_ref[(b // share) * nodes + n, :, j * size : (j + 1) * size] = value
        return carry

    lax.fori_loop(0, nodes, rows, 0)


def back_spread_kernel(per, width_k, nodes, pick, near, weight_ref, tiles_ref, *refs):
    parts, o_ref, p_ref, sums = refs[:nodes], refs[nodes], refs[nodes + 1], refs[nodes + 2 :]
    me = lax.axis_index("nodes")
    size = tiles_ref.shape[1]
    width = o_ref.shape[1]
    share = o_ref.shape[2] // size
    count = nodes * per
    block = [pl.multiple_of((me ^ i) * per, per) for i in range(nodes)]
    form_products(
        [(block[i], lambda i=i: parts[i][...]) for i in range(nodes)], count, width, tiles_ref, p_ref, True
    )
    for i in range(nodes):
        sums[0][pl.ds(block[i], per)] = parts[i][...].astype(f32).reshape(per, width, size)
    for total in sums[1:]:
        total[...] = jnp.zeros(total.shape, f32)

    def entry_row(r, carry):
        scale = weight_ref[pl.ds(r, 1), :]

        def chunk(c, inner):
            base = c * unroll
            for u in range(unroll):
                g = near[r, base + u]
                sums[u][g] = sums[u][g] + scale * p_ref[pick[r, base + u]]
            return inner

        return lax.fori_loop(0, (near[r, width_k] + (unroll - 1)) // unroll, chunk, carry)

    lax.fori_loop(0, count, entry_row, 0)

    def rows(n, carry):
        for b in range(per):
            r = n * per + b
            j = b % share
            value = ((sums[0][r] + sums[1][r]) + (sums[2][r] + sums[3][r])).astype(bf16)
            o_ref[(b // share) * nodes + n, :, j * size : (j + 1) * size] = value
        return carry

    lax.fori_loop(0, nodes, rows, 0)


def last_kernel(per, width_k, pick, weight_ref, v_ref, tiles_ref, o_ref, x_ref, p_ref):
    nodes = o_ref.shape[0]
    count, width, size = x_ref.shape
    share = v_ref.shape[2] // size
    for f in range(per // share):
        for n in range(nodes):
            for j in range(share):
                x_ref[n * per + f * share + j] = v_ref[f * nodes + n, :, j * size : (j + 1) * size]
    group = 256 // width
    lefts = [
        (first, lambda first=first: x_ref[first : first + group].reshape(group * width, size))
        for first in range(0, count, group)
    ]
    form_products(lefts, count, width, tiles_ref, p_ref, False)

    def rows(n, carry):
        for b in range(per):
            r = n * per + b
            acc = sum_entries(pick, r, width_k, p_ref)
            value = x_ref[r].astype(f32) + weight_ref[pl.ds(r, 1), :] * acc
            o_ref[n, :, b * size : (b + 1) * size] = value.astype(bf16)
        return carry

    lax.fori_loop(0, nodes, rows, 0)


def plain_spread(x, ids, tiles, transposed):
    near, tile_ids, degrees = ids
    rows = jnp.arange(x.shape[0])
    kind = "gfi,tij->tgfj" if transposed else "gfj,tij->tgfi"
    products = jnp.einsum(kind, x, tiles, preferred_element_type=f32)
    weight = lax.rsqrt(degrees.astype(f32))

    def step(k, acc):
        g, t = near[:, k], tile_ids[:, k]
        scale = jnp.where(k < degrees, weight, 0.0)[:, None, None]
        if transposed:
            return acc.at[g].add(scale * products[t, rows])
        return acc + scale * products[t, g]

    return lax.fori_loop(0, near.shape[1], step, x.astype(f32)).astype(bf16)


def product_flops(tiles, count, width):
    return 2 * tiles.shape[0] * count * width * tiles.shape[1] * tiles.shape[1]


def product_scratch(tiles, count, width):
    return pltpu.VMEM((tiles.shape[0] * count + 1, width, tiles.shape[1]), f32)


def spread_first(v, tiles, per, width_k, feat_count):
    nodes, rows, size = v.shape
    width = (rows - meta_rows) // per
    count, share = nodes * per, per // feat_count
    if width % 16:
        raw = v[:, rows - meta_rows :, :].astype(jnp.int32)
        links = raw[:, :per].reshape(count, size)
        ids = (links[:, :width_k], raw[:, per:].reshape(count, size)[:, :width_k], links[:, width_k])
        out = plain_spread(v[:, : rows - meta_rows].reshape(count, width, size), ids, tiles, False)
        out = out.reshape(nodes, feat_count, share, width, size).transpose(1, 0, 3, 2, 4)
        return out.reshape(feat_count * nodes, width, share * size), ids
    return_ids = ((3, count, size), jnp.int32)
    out, ids, weight = call(
        functools.partial(first_kernel, per, width_k),
        [((feat_count * nodes, width, share * size), bf16), return_ids, ((count, size), f32)],
        [far, vmem],
        (v, tiles),
        [
            pltpu.SMEM((count, size), jnp.int32),
            product_scratch(tiles, count, width),
            pltpu.SemaphoreType.DMA,
        ],
        0,
        28,
        sent=(0, 1, 2),
    )
    return out, (ids[0], ids[1], ids[2], weight)


def spread_back(parts, ids, tiles, per, width_k, feat_count):
    nodes, size = len(parts), tiles.shape[1]
    width, count, share = parts[0].shape[0] // per, len(parts) * per, per // feat_count
    if width % 16:
        order = lax.axis_index("nodes") ^ jnp.arange(nodes)
        out = plain_spread(jnp.stack(parts)[order].reshape(count, width, size), ids, tiles, True)
        out = out.reshape(nodes, feat_count, share, width, size).transpose(1, 0, 3, 2, 4)
        return out.reshape(feat_count * nodes, width, share * size)
    _, pick_back, near, weight = ids
    return call(
        functools.partial(back_spread_kernel, per, width_k, nodes),
        [((feat_count * nodes, width, share * size), bf16)],
        [smem, smem, vmem, vmem, vmem] + [far] * (nodes - 1),
        (pick_back, near, weight, tiles, *parts),
        [product_scratch(tiles, count, width)] + [pltpu.VMEM((count, width, size), f32)] * unroll,
        product_flops(tiles, count, width),
        28,
        4 << 20,
        (0,),
    )[0]


def spread_last(v, ids, tiles, per, width_k, nodes):
    size = tiles.shape[1]
    every, width, held = v.shape
    feat_count, share, count = every // nodes, held // size, nodes * per
    if width % 16:
        x = v.reshape(feat_count, nodes, width, share, size).transpose(1, 0, 3, 2, 4).reshape(count, width, size)
        out = plain_spread(x, ids, tiles, False)
        return out.reshape(nodes, per, width, size).transpose(0, 2, 1, 3).reshape(nodes, width, per * size)
    pick, _, _, weight = ids
    return call(
        functools.partial(last_kernel, per, width_k),
        [((nodes, width, per * size), bf16)],
        [smem, vmem, vmem, vmem],
        (pick, weight, v, tiles),
        [pltpu.VMEM((count, width, size), bf16), product_scratch(tiles, count, width)],
        10 * product_flops(tiles, count, width),
        28,
        sent=(0,),
    )[0]


def swap(values, axis, mask):
    return lax.ppermute(values, axis, [(i, i ^ mask) for i in range(lax.axis_size(axis))])


def gather_parts(values, axis):
    parts, offsets = [values], [0]
    bit = lax.axis_size(axis) // 2
    while bit:
        parts = parts + [swap(v, axis, bit) for v in parts]
        offsets = offsets + [o ^ bit for o in offsets]
        bit //= 2
    return parts, offsets


def project_kernel(offsets, agg_ref, *refs):
    count = len(offsets)
    weights, (pre_ref, hidden_ref, y_ref) = refs[:count], refs[count:]
    me = lax.axis_index("feat")
    wide = weights[0].shape[1]
    agg = agg_ref[...]
    place = [pl.ds(pl.multiple_of((me ^ o) * wide, wide), wide) for o in offsets]
    for at, w_ref in zip(place, weights):
        pre = jnp.dot(w_ref[0], agg, preferred_element_type=f32)
        pre_ref[at, :] = pre
        hidden_ref[at, :] = (pre * jax.nn.sigmoid(pre)).astype(bf16)
    hidden = hidden_ref[...]
    for at, w_ref in zip(place, weights):
        y_ref[at, :] = jnp.dot(w_ref[1], hidden, preferred_element_type=f32).astype(bf16)


def side_rows(left_ref, tall):
    side = lax.axis_index("nodes") % 2
    pick = lambda row: left_ref[pl.ds(pl.multiple_of(row * tall, tall), tall), :]
    half = left_ref.shape[0] // (2 * tall)
    return [jnp.concatenate([pick(2 * h + (side ^ b)) for h in range(half)], axis=0) for b in range(2)]


def give_blocks(left_ref, right_ref, outs, offsets):
    me = lax.axis_index("feat")
    half, tall, wide = outs[0].shape
    lefts = side_rows(left_ref, tall)
    for i, o in enumerate(offsets):
        right = right_ref[pl.ds(pl.multiple_of((me ^ o ^ 1) * wide, wide), wide), :]
        for b in range(2):
            outs[2 * i + b][...] = nt_dot(lefts[b], right).reshape(half, tall, wide).astype(bf16)


def product_kernel(offsets, left_ref, right_ref, *outs):
    give_blocks(left_ref, right_ref, outs, offsets)


def back_kernel(offsets, evens, pre_ref, back_ref, left_ref, *refs):
    count = len(offsets)
    weights, outs, out_ref = refs[:count], refs[count:-1], refs[-1]
    me = lax.axis_index("feat")
    wide = weights[0].shape[1]
    place = [pl.ds(pl.multiple_of((me ^ o) * wide, wide), wide) for o in offsets]
    for at in place:
        total = None
        for w_ref, rows in zip(weights, place):
            term = lax.dot_general(
                w_ref[1, :, at], back_ref[rows, :], (((0,), (0,)), ((), ())), preferred_element_type=f32
            )
            total = term if total is None else total + term
        pre = pre_ref[at, :]
        sigma = jax.nn.sigmoid(pre)
        out_ref[at, :] = (total * sigma * (1.0 + pre * (1.0 - sigma))).astype(bf16)
    give_blocks(left_ref, out_ref, outs, evens)


def quarter_kernel(offsets, left_ref, right_ref, *refs):
    spots = 2 * len(offsets)
    came, outs = refs[:spots], refs[spots:]
    me = lax.axis_index("feat")
    half, tall, wide = outs[0].shape
    lefts = side_rows(left_ref, tall)
    for i, o in enumerate(offsets):
        right = right_ref[pl.ds(pl.multiple_of((me ^ o) * wide, wide), wide), :]
        for b in range(2):
            total = nt_dot(lefts[b], right).reshape(half, tall, wide) + came[2 * i + b][...].astype(f32)
            outs[2 * i + b][...] = total.astype(outs[2 * i + b].dtype)


def split_kernel(keep_ref, *refs):
    half = keep_ref.shape[0]
    came, mine_ref, outs = refs[:-half], refs[-half], refs[len(refs) - half + 1 :]
    me = lax.axis_index("nodes") // 2
    for i, o_ref in enumerate((mine_ref,) + outs):
        total = keep_ref[me ^ i]
        for ref in came:
            total = total + ref[me ^ i].astype(f32)
        o_ref[...] = total.astype(o_ref.dtype)


def even_offsets():
    return list(range(0, lax.axis_size("feat"), 2))


def give_shapes(hidden_width):
    nodes, count = lax.axis_size("nodes"), lax.axis_size("feat")
    return [((nodes // 2, hidden_width // nodes, hidden_width // count), bf16)] * count


def quarters(left, right, *given):
    swapped = [swap(v, "feat", 1) for v in given]
    shape = given[0].shape
    return call(
        functools.partial(quarter_kernel, even_offsets()),
        [(shape, f32)] + [(shape, bf16)] * (len(given) - 1),
        [vmem] * (2 + len(given)),
        (left, right, *swapped),
        sent=tuple(range(1, len(given))),
    )


def pass_quarters(mine, *rest, late=None):
    nodes, feat_count = lax.axis_size("nodes"), lax.axis_size("feat")
    spots = [(o, b) for o in even_offsets() for b in range(2)][1:]
    ring = range(nodes * feat_count)
    if late is not None:
        rest = [after(v, late) if o == 0 else v for v, (o, b) in zip(rest, spots)]
    moved = [
        lax.ppermute(v, ("nodes", "feat"), [(i, i ^ (b * feat_count + o)) for i in ring]) for v, (o, b) in zip(rest, spots)
    ]
    return mine, *moved


def grad_sum(flops, keep, *came):
    half, tall, wide = keep.shape
    mine, *rest = call(
        split_kernel,
        [((tall, wide), f32)] + [((tall, wide), bf16)] * (half - 1),
        [vmem] * (1 + len(came)),
        (keep, *came),
        flops=flops,
        sent=tuple(range(1, half)),
    )
    for i, part in enumerate(rest):
        mine = mine + swap(part, "nodes", 2 * (i + 1)).astype(f32)
    return mine


def on_device(
    features, ghosts, slots, tile_ids, degrees, tile_table, weight_one, weight_two, cotangent
):
    nodes, feat_count = lax.axis_size("nodes"), lax.axis_size("feat")
    every = ("feat", "nodes")
    per, width_k = slots.shape
    size = tile_table.shape[1]
    rows, wide = features.shape
    held = rows // feat_count
    hidden_width = wide * feat_count
    exchange = lambda v, axes: lax.all_to_all(v, axes, split_axis=0, concat_axis=0, tiled=True)

    sent = pack(features, ghosts, slots, tile_ids, degrees, nodes, size)
    came = exchange(sent, "nodes")
    packed = pack_parts(after(cotangent, sent), nodes, size)
    first, second = after((weight_one, weight_two), sent)
    weights, offsets = gather_parts(jnp.stack([first.T, second.T]), "feat")

    spread, ids = spread_first(after(came, packed), tile_table, per, width_k, feat_count)
    cot_parts = [packed[0]] + [swap(p, "nodes", i) for i, p in enumerate(packed) if i]
    agg = exchange(after(spread, *cot_parts), every).reshape(hidden_width, held)
    back = spread_back(cot_parts, ids, tile_table, per, width_k, feat_count)
    agg = after(agg, back)
    back = exchange(back, every).reshape(hidden_width, held)

    parts = len(offsets)
    pre, hidden, wide_out = call(
        functools.partial(project_kernel, offsets),
        [((hidden_width, held), f32)] + [((hidden_width, held), bf16)] * 2,
        [vmem] * (1 + parts),
        (agg, *weights),
        flops=4 * hidden_width * hidden_width * held,
        moved=4 << 20,
        sent=(0, 2),
    )
    wide_out = after(wide_out, back)
    out_t = exchange(wide_out.reshape(feat_count * nodes, wide // nodes, held), every)

    evens = even_offsets()
    give_two = call(
        functools.partial(product_kernel, evens),
        give_shapes(hidden_width),
        [vmem] * 2,
        (hidden, back),
        sent=tuple(range(parts)),
    )
    *give_one, back_pre = call(
        functools.partial(back_kernel, offsets, evens),
        give_shapes(hidden_width) + [((hidden_width, held), bf16)],
        [far] + [vmem] * (2 + parts),
        (pre, back, agg, *weights),
        sent=tuple(range(parts)),
    )
    halves_two = quarters(hidden, back, *give_two)
    halves_one = quarters(agg, back_pre, *give_one)
    quarters_two = pass_quarters(*halves_two)
    last = spread_last(out_t, ids, tile_table, per, width_k, nodes)
    out_n = exchange(last, "nodes")
    quarters_one = pass_quarters(*halves_one, late=None)
    grad_two = grad_sum(0, *after(quarters_two, last))
    grad_one = grad_sum(20 << 30, *after(quarters_one, last))
    output = out_n.reshape(wide, rows).T
    return (output, grad_one, grad_two)


def solution(mesh):
    return jax.shard_map(
        on_device,
        mesh=mesh,
        in_specs=(
            P("nodes", "feat"),
            P("nodes", None),
            P("nodes", None),
            P("nodes", None),
            P("nodes"),
            P(),
            P(None, "feat"),
            P(None, "feat"),
            P("nodes", "feat"),
        ),
        out_specs=(P("nodes", "feat"), P("nodes", "feat"), P("nodes", "feat")),
        check_vma=False,
    )
```

```python
import functools

import jax
import jax.numpy as jnp
from jax import lax
from jax.experimental import pallas as pl
from jax.experimental.pallas import tpu as pltpu
from jax.sharding import PartitionSpec as P

unroll = 4
tile_step = 8
meta_rows = 16
bf16, f32 = jnp.bfloat16, jnp.float32
vmem = pl.BlockSpec(memory_space=pltpu.VMEM)
smem = pl.BlockSpec(memory_space=pltpu.SMEM)
far = object()


def nt_dot(a, b):
    return lax.dot_general(a, b, (((1,), (1,)), ((), ())), preferred_element_type=f32)


def call(body, outs, in_specs, args, scratch=(), flops=0, limit=16, moved=0, sent=()):
    return pl.pallas_call(
        body,
        out_shape=[(pltpu.HBM if i in sent else jax.ShapeDtypeStruct)(s, d) for i, (s, d) in enumerate(outs)],
        in_specs=[vmem if spec is far else spec for spec in in_specs],
        out_specs=[vmem] * len(outs),
        scratch_shapes=list(scratch),
        compiler_params=pltpu.CompilerParams(vmem_limit_bytes=limit * 1024 * 1024),
        cost_estimate=pl.CostEstimate(flops=flops, bytes_accessed=moved, transcendentals=0),
    )(*[pltpu.with_memory_space_constraint(v, pltpu.HBM) if spec is far else v for v, spec in zip(args, in_specs)])


def after(values, *earlier):
    return lax.optimization_barrier((values, earlier))[0]


def meta_tile(ghost_at, degree_at, slots, tile_ids, owners, held, size):
    per, width_k = slots.shape
    near = jnp.zeros((per, width_k), jnp.int32)
    for s in range(owners * held):
        near = jnp.where(slots == s, (s // held) * per + ghost_at(s // held, s % held), near)
    row = lax.broadcasted_iota(jnp.int32, (per, size), 0)
    lane = lax.broadcasted_iota(jnp.int32, (per, size), 1)
    degree = jnp.zeros((per, size), jnp.int32)
    for r in range(per):
        degree = jnp.where(row == r, degree_at(r), degree)
    widen = lambda v: jnp.concatenate([v, jnp.zeros((per, size - width_k), jnp.int32)], axis=1)
    top = jnp.where(lane == width_k, degree, widen(near))
    return jnp.concatenate([top, widen(tile_ids)], axis=0).astype(f32).astype(bf16)


def pack_kernel(owners, held, ghosts, degrees, slots_ref, tiles_ref, feat_ref, o_ref):
    nodes, rows, size = o_ref.shape
    width = feat_ref.shape[1] // nodes
    per = feat_ref.shape[0] // size
    for b in range(per):
        turned = feat_ref[b * size : (b + 1) * size, :].T
        for n in range(nodes):
            o_ref[n, b * width : (b + 1) * width, :] = turned[n * width : (n + 1) * width]
    tile = meta_tile(
        lambda p, c: ghosts[c : c + 1, p : p + 1], lambda r: degrees[r], slots_ref[...], tiles_ref[...], owners, held, size
    )
    for n in range(nodes):
        o_ref[n, rows - meta_rows :, :] = tile


def turn_blocks(values, nodes, size):
    per, width = values.shape[0] // size, values.shape[1] // nodes
    return values.reshape(per, size, nodes, width).transpose(2, 0, 3, 1).reshape(nodes, per * width, size)


def pack(features, ghosts, slots, tile_ids, degrees, nodes, size):
    owners, held = ghosts.shape
    per = slots.shape[0]
    width = features.shape[1] // nodes
    if width % 16:
        tile = meta_tile(lambda p, c: ghosts[p, c], lambda r: degrees[r], slots, tile_ids, owners, held, size)
        tile = jnp.broadcast_to(tile, (nodes,) + tile.shape)
        return jnp.concatenate([turn_blocks(features, nodes, size), tile], axis=1)
    return call(
        functools.partial(pack_kernel, owners, held),
        [((nodes, per * width + meta_rows, size), bf16)],
        [far, smem, far, far, far],
        (ghosts.T, pltpu.with_memory_space_constraint(degrees, pltpu.HBM), slots, tile_ids, features),
        sent=(0,),
    )[0]


def turn_kernel(v_ref, *refs):
    outs, turned_ref = refs[:-1], refs[-1]
    size = outs[0].shape[1]
    per = v_ref.shape[0] // size
    width = v_ref.shape[1] // len(outs)
    me = lax.axis_index("nodes")
    for b in range(per):
        turned_ref[b] = v_ref[b * size : (b + 1) * size, :].T
    for i, o_ref in enumerate(outs):
        at = pl.ds(pl.multiple_of((me ^ i) * width, width), width)
        for b in range(per):
            o_ref[b * width : (b + 1) * width, :] = turned_ref[b, at, :]


def pack_parts(values, nodes, size):
    per, width = values.shape[0] // size, values.shape[1] // nodes
    if width % 16:
        me = lax.axis_index("nodes")
        turned = turn_blocks(values, nodes, size)
        return [lax.dynamic_index_in_dim(turned, me ^ i, 0, keepdims=False) for i in range(nodes)]
    return call(
        turn_kernel,
        [((per * width, size), bf16)] * nodes,
        [vmem],
        (values,),
        [pltpu.VMEM((per, values.shape[1], size), bf16)],
        sent=tuple(range(nodes)),
    )


def form_products(lefts, count, width, tiles_ref, p_ref, transposed):
    tile_count, size = tiles_ref.shape[0], tiles_ref.shape[1]

    def step(turn, carry):
        some = tiles_ref[pl.ds(tile_step * turn, tile_step)]
        if transposed:
            right = jnp.concatenate([some[i] for i in range(tile_step)], axis=1)
        else:
            right = some.reshape(tile_step * size, size)
        for first, load in lefts:
            left = load()
            res = jnp.dot(left, right, preferred_element_type=f32) if transposed else nt_dot(left, right)
            group = left.shape[0] // width
            for i in range(tile_step):
                part = res[:, i * size : (i + 1) * size].reshape(group, width, size)
                p_ref[pl.ds((tile_step * turn + i) * count + first, group)] = part
        return carry

    lax.fori_loop(0, tile_count // tile_step, step, 0)
    p_ref[tile_count * count] = jnp.zeros((width, size), f32)


def sum_entries(pick, r, width_k, p_ref):
    terms = [p_ref[pick[r, k]] for k in range(width_k)]
    while len(terms) > 1:
        terms = [terms[i] + terms[i + 1] for i in range(0, len(terms) - 1, 2)] + terms[len(terms) & ~1 :]
    return terms[0]


def first_kernel(per, width_k, v_ref, tiles_ref, o_ref, ids_ref, weight_ref, pick, p_ref, sem):
    nodes, _, size = v_ref.shape
    width = o_ref.shape[1]
    share = o_ref.shape[2] // size
    count = nodes * per
    span = per * width
    empty = tiles_ref.shape[0] * count
    lane = lax.broadcasted_iota(jnp.int32, (per, size), 1)
    row = lax.broadcasted_iota(jnp.int32, (per, size), 0)
    for n in range(nodes):
        raw = v_ref[n, span:, :].astype(f32).astype(jnp.int32)
        links, tile = raw[:per], raw[per:]
        degree = jnp.broadcast_to(links[:, width_k : width_k + 1], (per, size))
        live = lane < degree
        block = slice(n * per, (n + 1) * per)
        ids_ref[0, block] = jnp.where(live, tile * count + links, empty)
        ids_ref[1, block] = jnp.where(live, tile * count + (row + n * per), empty)
        ids_ref[2, block] = links
        weight_ref[block] = lax.rsqrt(degree.astype(f32))
    copy = pltpu.make_async_copy(ids_ref.at[0], pick, sem)
    copy.start()
    lefts = [(n * per, lambda n=n: v_ref[n, :span, :]) for n in range(nodes)]
    form_products(lefts, count, width, tiles_ref, p_ref, False)
    copy.wait()

    def rows(n, carry):
        for b in range(per):
            r = n * per + b
            own = v_ref[n, b * width : (b + 1) * width, :].astype(f32)
            j = b % share
            value = (own + weight_ref[pl.ds(r, 1), :] * sum_entries(pick, r, width_k, p_ref)).astype(bf16)
            o_ref[(b // share) * nodes + n, :, j * size : (j + 1) * size] = value
        return carry

    lax.fori_loop(0, nodes, rows, 0)


def back_spread_kernel(per, width_k, nodes, pick, near, weight_ref, tiles_ref, *refs):
    parts, o_ref, p_ref, sums = refs[:nodes], refs[nodes], refs[nodes + 1], refs[nodes + 2 :]
    me = lax.axis_index("nodes")
    size = tiles_ref.shape[1]
    width = o_ref.shape[1]
    share = o_ref.shape[2] // size
    count = nodes * per
    block = [pl.multiple_of((me ^ i) * per, per) for i in range(nodes)]
    form_products(
        [(block[i], lambda i=i: parts[i][...]) for i in range(nodes)], count, width, tiles_ref, p_ref, True
    )
    for i in range(nodes):
        sums[0][pl.ds(block[i], per)] = parts[i][...].astype(f32).reshape(per, width, size)
    for total in sums[1:]:
        total[...] = jnp.zeros(total.shape, f32)

    def entry_row(r, carry):
        scale = weight_ref[pl.ds(r, 1), :]

        def chunk(c, inner):
            base = c * unroll
            for u in range(unroll):
                g = near[r, base + u]
                sums[u][g] = sums[u][g] + scale * p_ref[pick[r, base + u]]
            return inner

        return lax.fori_loop(0, (near[r, width_k] + (unroll - 1)) // unroll, chunk, carry)

    lax.fori_loop(0, count, entry_row, 0)

    def rows(n, carry):
        for b in range(per):
            r = n * per + b
            j = b % share
            value = ((sums[0][r] + sums[1][r]) + (sums[2][r] + sums[3][r])).astype(bf16)
            o_ref[(b // share) * nodes + n, :, j * size : (j + 1) * size] = value
        return carry

    lax.fori_loop(0, nodes, rows, 0)


def last_kernel(per, width_k, pick, weight_ref, v_ref, tiles_ref, o_ref, x_ref, p_ref):
    nodes = o_ref.shape[0]
    count, width, size = x_ref.shape
    share = v_ref.shape[2] // size
    for f in range(per // share):
        for n in range(nodes):
            for j in range(share):
                x_ref[n * per + f * share + j] = v_ref[f * nodes + n, :, j * size : (j + 1) * size]
    group = 256 // width
    lefts = [
        (first, lambda first=first: x_ref[first : first + group].reshape(group * width, size))
        for first in range(0, count, group)
    ]
    form_products(lefts, count, width, tiles_ref, p_ref, False)

    def rows(n, carry):
        for b in range(per):
            r = n * per + b
            acc = sum_entries(pick, r, width_k, p_ref)
            value = x_ref[r].astype(f32) + weight_ref[pl.ds(r, 1), :] * acc
            o_ref[n, :, b * size : (b + 1) * size] = value.astype(bf16)
        return carry

    lax.fori_loop(0, nodes, rows, 0)


def plain_spread(x, ids, tiles, transposed):
    near, tile_ids, degrees = ids
    rows = jnp.arange(x.shape[0])
    kind = "gfi,tij->tgfj" if transposed else "gfj,tij->tgfi"
    products = jnp.einsum(kind, x, tiles, preferred_element_type=f32)
    weight = lax.rsqrt(degrees.astype(f32))

    def step(k, acc):
        g, t = near[:, k], tile_ids[:, k]
        scale = jnp.where(k < degrees, weight, 0.0)[:, None, None]
        if transposed:
            return acc.at[g].add(scale * products[t, rows])
        return acc + scale * products[t, g]

    return lax.fori_loop(0, near.shape[1], step, x.astype(f32)).astype(bf16)


def product_flops(tiles, count, width):
    return 2 * tiles.shape[0] * count * width * tiles.shape[1] * tiles.shape[1]


def product_scratch(tiles, count, width):
    return pltpu.VMEM((tiles.shape[0] * count + 1, width, tiles.shape[1]), f32)


def spread_first(v, tiles, per, width_k, feat_count):
    nodes, rows, size = v.shape
    width = (rows - meta_rows) // per
    count, share = nodes * per, per // feat_count
    if width % 16:
        raw = v[:, rows - meta_rows :, :].astype(jnp.int32)
        links = raw[:, :per].reshape(count, size)
        ids = (links[:, :width_k], raw[:, per:].reshape(count, size)[:, :width_k], links[:, width_k])
        out = plain_spread(v[:, : rows - meta_rows].reshape(count, width, size), ids, tiles, False)
        out = out.reshape(nodes, feat_count, share, width, size).transpose(1, 0, 3, 2, 4)
        return out.reshape(feat_count * nodes, width, share * size), ids
    return_ids = ((3, count, size), jnp.int32)
    out, ids, weight = call(
        functools.partial(first_kernel, per, width_k),
        [((feat_count * nodes, width, share * size), bf16), return_ids, ((count, size), f32)],
        [far, vmem],
        (v, tiles),
        [
            pltpu.SMEM((count, size), jnp.int32),
            product_scratch(tiles, count, width),
            pltpu.SemaphoreType.DMA,
        ],
        0,
        28,
        sent=(0, 1, 2),
    )
    return out, (ids[0], ids[1], ids[2], weight)


def spread_back(parts, ids, tiles, per, width_k, feat_count):
    nodes, size = len(parts), tiles.shape[1]
    width, count, share = parts[0].shape[0] // per, len(parts) * per, per // feat_count
    if width % 16:
        order = lax.axis_index("nodes") ^ jnp.arange(nodes)
        out = plain_spread(jnp.stack(parts)[order].reshape(count, width, size), ids, tiles, True)
        out = out.reshape(nodes, feat_count, share, width, size).transpose(1, 0, 3, 2, 4)
        return out.reshape(feat_count * nodes, width, share * size)
    _, pick_back, near, weight = ids
    return call(
        functools.partial(back_spread_kernel, per, width_k, nodes),
        [((feat_count * nodes, width, share * size), bf16)],
        [smem, smem, vmem, vmem, vmem] + [far] * (nodes - 1),
        (pick_back, near, weight, tiles, *parts),
        [product_scratch(tiles, count, width)] + [pltpu.VMEM((count, width, size), f32)] * unroll,
        product_flops(tiles, count, width),
        28,
        4 << 20,
        (0,),
    )[0]


def spread_last(v, ids, tiles, per, width_k, nodes):
    size = tiles.shape[1]
    every, width, held = v.shape
    feat_count, share, count = every // nodes, held // size, nodes * per
    if width % 16:
        x = v.reshape(feat_count, nodes, width, share, size).transpose(1, 0, 3, 2, 4).reshape(count, width, size)
        out = plain_spread(x, ids, tiles, False)
        return out.reshape(nodes, per, width, size).transpose(0, 2, 1, 3).reshape(nodes, width, per * size)
    pick, _, _, weight = ids
    return call(
        functools.partial(last_kernel, per, width_k),
        [((nodes, width, per * size), bf16)],
        [smem, vmem, vmem, vmem],
        (pick, weight, v, tiles),
        [pltpu.VMEM((count, width, size), bf16), product_scratch(tiles, count, width)],
        10 * product_flops(tiles, count, width),
        28,
        sent=(0,),
    )[0]


def swap(values, axis, mask):
    return lax.ppermute(values, axis, [(i, i ^ mask) for i in range(lax.axis_size(axis))])


def gather_parts(values, axis):
    parts, offsets = [values], [0]
    bit = lax.axis_size(axis) // 2
    while bit:
        parts = parts + [swap(v, axis, bit) for v in parts]
        offsets = offsets + [o ^ bit for o in offsets]
        bit //= 2
    return parts, offsets


def project_kernel(offsets, agg_ref, *refs):
    count = len(offsets)
    weights, (pre_ref, hidden_ref, y_ref) = refs[:count], refs[count:]
    me = lax.axis_index("feat")
    wide = weights[0].shape[1]
    agg = agg_ref[...]
    place = [pl.ds(pl.multiple_of((me ^ o) * wide, wide), wide) for o in offsets]
    for at, w_ref in zip(place, weights):
        pre = jnp.dot(w_ref[0], agg, preferred_element_type=f32)
        pre_ref[at, :] = pre
        hidden_ref[at, :] = (pre * jax.nn.sigmoid(pre)).astype(bf16)
    hidden = hidden_ref[...]
    for at, w_ref in zip(place, weights):
        y_ref[at, :] = jnp.dot(w_ref[1], hidden, preferred_element_type=f32).astype(bf16)


def side_rows(left_ref, tall):
    side = lax.axis_index("nodes") % 2
    pick = lambda row: left_ref[pl.ds(pl.multiple_of(row * tall, tall), tall), :]
    half = left_ref.shape[0] // (2 * tall)
    return [jnp.concatenate([pick(2 * h + (side ^ b)) for h in range(half)], axis=0) for b in range(2)]


def give_blocks(left_ref, right_ref, outs, offsets):
    me = lax.axis_index("feat")
    half, tall, wide = outs[0].shape
    lefts = side_rows(left_ref, tall)
    for i, o in enumerate(offsets):
        right = right_ref[pl.ds(pl.multiple_of((me ^ o ^ 1) * wide, wide), wide), :]
        for b in range(2):
            outs[2 * i + b][...] = nt_dot(lefts[b], right).reshape(half, tall, wide).astype(bf16)


def product_kernel(offsets, left_ref, right_ref, *outs):
    give_blocks(left_ref, right_ref, outs, offsets)


def back_kernel(offsets, evens, pre_ref, back_ref, left_ref, *refs):
    count = len(offsets)
    weights, outs, out_ref = refs[:count], refs[count:-1], refs[-1]
    me = lax.axis_index("feat")
    wide = weights[0].shape[1]
    place = [pl.ds(pl.multiple_of((me ^ o) * wide, wide), wide) for o in offsets]
    for at in place:
        total = None
        for w_ref, rows in zip(weights, place):
            term = lax.dot_general(
                w_ref[1, :, at], back_ref[rows, :], (((0,), (0,)), ((), ())), preferred_element_type=f32
            )
            total = term if total is None else total + term
        pre = pre_ref[at, :]
        sigma = jax.nn.sigmoid(pre)
        out_ref[at, :] = (total * sigma * (1.0 + pre * (1.0 - sigma))).astype(bf16)
    give_blocks(left_ref, out_ref, outs, evens)


def quarter_kernel(offsets, left_ref, right_ref, *refs):
    spots = 2 * len(offsets)
    came, outs = refs[:spots], refs[spots:]
    me = lax.axis_index("feat")
    half, tall, wide = outs[0].shape
    lefts = side_rows(left_ref, tall)
    for i, o in enumerate(offsets):
        right = right_ref[pl.ds(pl.multiple_of((me ^ o) * wide, wide), wide), :]
        for b in range(2):
            total = nt_dot(lefts[b], right).reshape(half, tall, wide) + came[2 * i + b][...].astype(f32)
            outs[2 * i + b][...] = total.astype(outs[2 * i + b].dtype)


def split_kernel(keep_ref, *refs):
    half = keep_ref.shape[0]
    came, mine_ref, outs = refs[:-half], refs[-half], refs[len(refs) - half + 1 :]
    me = lax.axis_index("nodes") // 2
    for i, o_ref in enumerate((mine_ref,) + outs):
        total = keep_ref[me ^ i]
        for ref in came:
            total = total + ref[me ^ i].astype(f32)
        o_ref[...] = total.astype(o_ref.dtype)


def even_offsets():
    return list(range(0, lax.axis_size("feat"), 2))


def give_shapes(hidden_width):
    nodes, count = lax.axis_size("nodes"), lax.axis_size("feat")
    return [((nodes // 2, hidden_width // nodes, hidden_width // count), bf16)] * count


def quarters(left, right, *given):
    swapped = [swap(v, "feat", 1) for v in given]
    shape = given[0].shape
    return call(
        functools.partial(quarter_kernel, even_offsets()),
        [(shape, f32)] + [(shape, bf16)] * (len(given) - 1),
        [vmem] * (2 + len(given)),
        (left, right, *swapped),
        sent=tuple(range(1, len(given))),
    )


def pass_quarters(mine, *rest, late=None):
    nodes, feat_count = lax.axis_size("nodes"), lax.axis_size("feat")
    spots = [(o, b) for o in even_offsets() for b in range(2)][1:]
    ring = range(nodes * feat_count)
    if late is not None:
        rest = [after(v, late) if o == 0 else v for v, (o, b) in zip(rest, spots)]
    moved = [
        lax.ppermute(v, ("nodes", "feat"), [(i, i ^ (b * feat_count + o)) for i in ring]) for v, (o, b) in zip(rest, spots)
    ]
    return mine, *moved


def grad_sum(flops, keep, *came):
    half, tall, wide = keep.shape
    mine, *rest = call(
        split_kernel,
        [((tall, wide), f32)] + [((tall, wide), bf16)] * (half - 1),
        [vmem] * (1 + len(came)),
        (keep, *came),
        flops=flops,
        sent=tuple(range(1, half)),
    )
    for i, part in enumerate(rest):
        mine = mine + swap(part, "nodes", 2 * (i + 1)).astype(f32)
    return mine


def halving_kernel(keep_ref, *refs):
    came, kept_ref, give_ref = refs[:-2], refs[-2], refs[-1]
    me = lax.axis_index("nodes") // 2
    for i in range(kept_ref.shape[0]):
        for o_ref, to in ((kept_ref, me ^ (2 * i)), (give_ref, me ^ (2 * i) ^ 1)):
            total = keep_ref[to]
            for ref in came:
                total = total + ref[to].astype(f32)
            o_ref[i] = total.astype(o_ref.dtype)


def grad_sum_halving(flops, keep, *came):
    half, tall, wide = keep.shape
    kept, give = call(
        halving_kernel,
        [((half // 2, tall, wide), f32), ((half // 2, tall, wide), bf16)],
        [vmem] * (1 + len(came)),
        (keep, *came),
        flops=flops,
        sent=(1,),
    )
    bit = 1
    while True:
        total = kept + swap(give, "nodes", 2 * bit).astype(f32)
        if total.shape[0] == 1:
            return total[0]
        pairs = total.reshape(total.shape[0] // 2, 2, tall, wide)
        kept, give = pairs[:, 0], pairs[:, 1].astype(bf16)
        bit *= 2


def on_device(
    features, ghosts, slots, tile_ids, degrees, tile_table, weight_one, weight_two, cotangent
):
    nodes, feat_count = lax.axis_size("nodes"), lax.axis_size("feat")
    every = ("feat", "nodes")
    per, width_k = slots.shape
    size = tile_table.shape[1]
    rows, wide = features.shape
    held = rows // feat_count
    hidden_width = wide * feat_count
    exchange = lambda v, axes: lax.all_to_all(v, axes, split_axis=0, concat_axis=0, tiled=True)

    sent = pack(features, ghosts, slots, tile_ids, degrees, nodes, size)
    came = exchange(sent, "nodes")
    packed = pack_parts(after(cotangent, sent), nodes, size)
    first, second = after((weight_one, weight_two), sent)
    weights, offsets = gather_parts(jnp.stack([first.T, second.T]), "feat")

    spread, ids = spread_first(after(came, packed), tile_table, per, width_k, feat_count)
    cot_parts = [packed[0]] + [swap(p, "nodes", i) for i, p in enumerate(packed) if i]
    agg = exchange(after(spread, *cot_parts), every).reshape(hidden_width, held)
    back = spread_back(cot_parts, ids, tile_table, per, width_k, feat_count)
    agg = after(agg, back)
    back = exchange(back, every).reshape(hidden_width, held)

    parts = len(offsets)
    pre, hidden, wide_out = call(
        functools.partial(project_kernel, offsets),
        [((hidden_width, held), f32)] + [((hidden_width, held), bf16)] * 2,
        [vmem] * (1 + parts),
        (agg, *weights),
        flops=4 * hidden_width * hidden_width * held,
        moved=4 << 20,
        sent=(0, 2),
    )
    wide_out = after(wide_out, back)
    out_t = exchange(wide_out.reshape(feat_count * nodes, wide // nodes, held), every)

    evens = even_offsets()
    give_two = call(
        functools.partial(product_kernel, evens),
        give_shapes(hidden_width),
        [vmem] * 2,
        (hidden, back),
        sent=tuple(range(parts)),
    )
    *give_one, back_pre = call(
        functools.partial(back_kernel, offsets, evens),
        give_shapes(hidden_width) + [((hidden_width, held), bf16)],
        [far] + [vmem] * (2 + parts),
        (pre, back, agg, *weights),
        sent=tuple(range(parts)),
    )
    halves_two = quarters(hidden, back, *give_two)
    halves_one = quarters(agg, back_pre, *give_one)
    quarters_two = pass_quarters(*halves_two)
    last = spread_last(out_t, ids, tile_table, per, width_k, nodes)
    out_n = exchange(last, "nodes")
    quarters_one = pass_quarters(*halves_one, late=None)
    grad_two = grad_sum_halving(0, *after(quarters_two, last))
    grad_one = grad_sum_halving(20 << 30, *after(quarters_one, last))
    output = out_n.reshape(wide, rows).T
    return (output, grad_one, grad_two)


def solution(mesh):
    return jax.shard_map(
        on_device,
        mesh=mesh,
        in_specs=(
            P("nodes", "feat"),
            P("nodes", None),
            P("nodes", None),
            P("nodes", None),
            P("nodes"),
            P(),
            P(None, "feat"),
            P(None, "feat"),
            P("nodes", "feat"),
        ),
        out_specs=(P("nodes", "feat"), P("nodes", "feat"), P("nodes", "feat")),
        check_vma=False,
    )
```
